256 devices in a mesh: tok: 8 (over x, core), vocab: 32 (over z, y).
Axes of the slice: x: 4, y: 4, z: 8, core: 2. Of those that a mesh axis runs over, the one named last changes fastest.
Arguments:
- policy_hidden: bfloat16 [512, 5120], P(('tok', 'vocab')), may hold values from -15 to 15
- reference_hidden: bfloat16 [512, 5120], P(('tok', 'vocab')), may hold values from -15 to 15
- head_weight: bfloat16 [5120, 131072], P(None, ('tok', 'vocab')), may hold values from -1.118034 to 1.118034
- pair_map: int32 [512], replicated, may hold values from 0 to 511, each once
- response_mask: int32 [512], P(('tok', 'vocab')), may hold values 0 or 1
Outputs:
- token_divergence: float32 [512], P(('tok', 'vocab'))
- hidden_grad: bfloat16 [512, 5120], P(('tok', 'vocab'))
The draws below stay inside these ranges and needn't reach their ends.
Inputs may be any that keep to these rules, and one draw needn't show every extreme that they name: pair_map is a permutation of the 512 rows.
All inputs are finite; a program needn't handle non-finite values. No bound on the sum of `response_mask` on one device may be relied on, other than what follows from the above.
Results may differ from the reference program's by a relative error of at most 0.015.
Values may be sent and summed in bfloat16 or wider, within the bound.
No kernel may reach another device: no remote copies, remote signals or barrier semaphores. Data moves between devices by JAX's collectives and lax.ppermute only.
A program may use at most 128 MiB of HBM per device.

```python
import math
import jax
import jax.numpy as jnp
from jax import lax

D = 5120
VOCAB = 131072
TOKENS = 512


def draw_head_weight(key, part):
    key = jax.random.fold_in(key, 11)
    subkeys = jax.random.split(key, 1)
    position = jnp.arange(VOCAB).astype(jnp.float32)
    column_scale = 2.7 + 0.6 * position / VOCAB
    weights = jnp.clip(jax.random.normal(subkeys[0], (D, VOCAB)), -6.0, 6.0) * (column_scale / math.sqrt(D))[None, :]
    return weights.astype(jnp.bfloat16)


def draw_policy_hidden(key, part):
    key = jax.random.fold_in(key, 21)
    subkeys = jax.random.split(key, 1)
    hidden_rows = jnp.clip(jax.random.normal(subkeys[0], (TOKENS, D)), -6.0, 6.0)
    return hidden_rows.astype(jnp.bfloat16)


def draw_reference_hidden(key, part):
    key = jax.random.fold_in(key, 31)
    subkeys = jax.random.split(key, 1)
    hidden_rows = jnp.clip(jax.random.normal(subkeys[0], (TOKENS, D)), -6.0, 6.0)
    return hidden_rows.astype(jnp.bfloat16)


def plant(array, stream_key, least, top_value):
    spot = [jax.random.randint(jax.random.fold_in(stream_key, axis), (), 0, length) for axis, length in enumerate(array.shape)]
    longest = array.shape.index(max(array.shape))
    beside = spot[:longest] + [(spot[longest] + 1) % array.shape[longest]] + spot[longest + 1:]
    return array.at[tuple(spot)].set(least).at[tuple(beside)].set(top_value)


def setup_inputs(seed: int = 0) -> dict:
    splits = jax.random.split(jax.random.key(seed), 6)
    policy_hidden = draw_policy_hidden(jax.random.fold_in(splits[5], 71), 0)
    reference_hidden = draw_reference_hidden(jax.random.fold_in(splits[5], 71), 0)
    head_weight = draw_head_weight(jax.random.fold_in(splits[5], 71), 0)
    pair_map = jax.random.permutation(splits[3], TOKENS).astype(jnp.int32)
    response_mask = plant((jax.random.randint(splits[4], (TOKENS,), 0, 8) < 7).astype(jnp.int32), jax.random.fold_in(splits[4], 1), 0, 1)
    return {"policy_hidden": policy_hidden, "reference_hidden": reference_hidden, "head_weight": head_weight, "pair_map": pair_map, "response_mask": response_mask}


def log_total(logits):
    row_peak = jnp.max(logits, axis=1)
    return row_peak + jnp.log(jnp.sum(jnp.exp(logits - row_peak[:, None]), axis=1))


def block_terms(row_pair, head_weight):
    policy_rows, paired_rows = row_pair
    policy_logits = jnp.dot(policy_rows, head_weight, preferred_element_type=jnp.float32)
    reference_logits = jnp.dot(paired_rows, head_weight, preferred_element_type=jnp.float32)
    policy_lognorm = log_total(policy_logits)
    reference_lognorm = log_total(reference_logits)
    log_ratio = (policy_logits - policy_lognorm[:, None]) - (reference_logits - reference_lognorm[:, None])
    token_probs = jnp.exp(policy_logits - policy_lognorm[:, None])
    divergence = jnp.sum(token_probs * log_ratio, axis=1)
    logit_grad = (token_probs * (log_ratio - divergence[:, None])).astype(jnp.bfloat16)
    grad_rows = lax.dot_general(logit_grad, head_weight, (((1,), (1,)), ((), ())), preferred_element_type=jnp.float32)
    return divergence, grad_rows


def reference(policy_hidden, reference_hidden, head_weight, pair_map, response_mask):
    paired_hidden = jnp.take(reference_hidden, pair_map.astype(jnp.int32), axis=0)
    block_rows = 32
    block_count = TOKENS // block_rows
    policy_blocks = policy_hidden.reshape(block_count, block_rows, D)
    paired_blocks = paired_hidden.reshape(block_count, block_rows, D)
    divergence, grad_rows = lax.map(lambda row_pair: block_terms(row_pair, head_weight), (policy_blocks, paired_blocks))
    divergence = divergence.reshape(TOKENS)
    grad_rows = grad_rows.reshape(TOKENS, D)
    weight = response_mask.astype(jnp.float32)
    token_divergence = weight * divergence
    hidden_grad = (weight[:, None] * grad_rows).astype(jnp.bfloat16)
    return (token_divergence, hidden_grad)
```

```python
import jax
import jax.numpy as jnp
from jax import lax
from jax.sharding import PartitionSpec as P

X, CORES, Z, Y = 4, 2, 8, 4
F32, BF16 = jnp.float32, jnp.bfloat16


def flat(x, c, z, y):
    return ((x * CORES + c) * Z + z) * Y + y


def exchange(value, partner):
    pairs = [
        (flat(x, c, z, y), flat(*partner(x, c, z, y)))
        for x in range(X)
        for c in range(CORES)
        for z in range(Z)
        for y in range(Y)
    ]
    return lax.ppermute(value, ("tok", "vocab"), pairs)


def along_x(first, second):
    return lambda x, c, z, y: (x ^ (second if c else first), c, z, y)


def along_y(first, second):
    return lambda x, c, z, y: (x, c, z, y ^ (second if c else first))


def along_z(step):
    return lambda x, c, z, y: (x, c, z ^ step, y)


def across_cores(x, c, z, y):
    return (x, 1 - c, z, y)


Z_STEPS = (1, 2, 6)


def gray(j):
    return j ^ (j >> 1)


def z_slot(j):
    return j ^ ((j >> 2) << 1)


def gather_z(rows):
    for step in Z_STEPS:
        rows = jnp.concatenate([rows, exchange(rows, along_z(step))], 0)
    return rows


def gather_ring(rows, along, second_core):
    count = rows.shape[0]
    near = exchange(rows, along(1, 3))
    far = exchange(jnp.concatenate([rows, near], 0), along(3, 1))
    return jnp.concatenate(
        [
            rows,
            jnp.where(second_core, far[:count], near),
            jnp.where(second_core, near, far[:count]),
            far[count:],
        ],
        0,
    )


def scatter_step(total, partner):
    half = total.shape[0] // 2
    return total[:half] + exchange(total[half:].astype(BF16), partner).astype(F32)


def merge(a, b):
    policy_peak = jnp.maximum(a[0], b[0])
    reference_peak = jnp.maximum(a[1], b[1])
    pa, pb = jnp.exp(a[0] - policy_peak), jnp.exp(b[0] - policy_peak)
    ra, rb = jnp.exp(a[1] - reference_peak), jnp.exp(b[1] - reference_peak)
    return jnp.stack(
        [
            policy_peak,
            reference_peak,
            a[2] * pa + b[2] * pb,
            a[3] * ra + b[3] * rb,
            a[4] * pa + b[4] * pb,
        ]
    )


def on_device(policy_hidden, reference_hidden, head_weight, pair_map, response_mask):
    tok, vocab = lax.axis_index("tok"), lax.axis_index("vocab")
    x0, c0, z0, y0 = tok // CORES, tok % CORES, vocab // Y, vocab % Y
    second = c0 == 1
    own_rows, width = policy_hidden.shape
    half = width // 2
    columns = head_weight.shape[1]
    chip_rows = CORES * own_rows
    tokens = X * Y * Z * chip_rows
    mine = tokens // 2

    own = jnp.concatenate([policy_hidden, reference_hidden], 0)
    keep = lax.dynamic_slice_in_dim(own, c0 * half, half, 1)
    got = exchange(lax.dynamic_slice_in_dim(own, (1 - c0) * half, half, 1), across_cores)
    first_rows = jnp.where(second, got, keep)
    second_rows = jnp.where(second, keep, got)
    rows = jnp.concatenate(
        [first_rows[:own_rows], second_rows[:own_rows], first_rows[own_rows:], second_rows[own_rows:]], 0
    )
    head_keep = lax.dynamic_slice_in_dim(head_weight, c0 * half, half, 0)
    head_got = exchange(lax.dynamic_slice_in_dim(head_weight, (1 - c0) * half, half, 0), across_cores)
    head = jnp.concatenate([head_keep, head_got], 1)

    rows = gather_z(rows).reshape(Z, 2, chip_rows, half)
    policy = rows[:, 0].reshape(Z * chip_rows, half)
    paired = rows[:, 1].reshape(Z * chip_rows, half)
    policy = gather_ring(policy, along_x, second)
    paired = gather_ring(paired, along_y, second)
    policy = gather_ring(policy, along_y, second)
    paired = gather_ring(paired, along_x, second)

    slot = jnp.arange(tokens, dtype=jnp.int32)
    sr, sc = slot % own_rows, (slot // own_rows) % CORES
    sz = z_slot((slot // chip_rows) % Z) ^ z0
    sx = gray((slot // (chip_rows * Z)) % X) ^ x0
    sy = gray(slot // (chip_rows * Z * X)) ^ y0
    partner = jnp.take(pair_map, flat(sx, sc, sz, sy) * own_rows + sr, axis=0)
    pr, pdev = partner % own_rows, partner // own_rows
    py, pz, pc, px = pdev % Y, (pdev // Y) % Z, (pdev // (Y * Z)) % CORES, pdev // (Y * Z * CORES)
    place = (((gray(px ^ x0) * Y + gray(py ^ y0)) * Z + z_slot(pz ^ z0)) * CORES + pc) * own_rows + pr
    one_hot = (place[:, None] == jnp.arange(tokens, dtype=jnp.int32)[None]).astype(BF16)
    paired = jnp.dot(one_hot, paired, preferred_element_type=F32).astype(BF16)

    policy_part = jnp.dot(policy, head, preferred_element_type=F32)
    reference_part = jnp.dot(paired, head, preferred_element_type=F32)

    def finish(part):
        keep = lax.dynamic_slice_in_dim(part, c0 * mine, mine, 0)
        send = lax.dynamic_slice_in_dim(part, (1 - c0) * mine, mine, 0)
        got = exchange(send, across_cores)
        return keep + jnp.concatenate([got[:, columns:], got[:, :columns]], 1)

    policy_logits = finish(policy_part)
    reference_logits = finish(reference_part)
    difference = policy_logits - reference_logits

    policy_peak = jnp.max(policy_logits, axis=1)
    reference_peak = jnp.max(reference_logits, axis=1)
    policy_exp = jnp.exp(policy_logits - policy_peak[:, None])
    reference_exp = jnp.exp(reference_logits - reference_peak[:, None])
    stats = jnp.stack(
        [
            policy_peak,
            reference_peak,
            jnp.sum(policy_exp, axis=1),
            jnp.sum(reference_exp, axis=1),
            jnp.sum(policy_exp * difference, axis=1),
        ]
    )
    order = (5, 2, 2, 2, 2, 2, 2, chip_rows)
    for partner_of, bit in (
        (along_z(1), 6),
        (along_z(2), 5),
        (along_z(6), 4),
        (along_x(1, 1), 3),
        (along_x(3, 3), 2),
        (along_y(1, 1), 1),
        (lambda x, c, z, y: (x, 1 - c, z, y ^ 3), None),
    ):
        other = exchange(stats, partner_of)
        if bit is not None:
            other = jnp.flip(other.reshape(order), bit).reshape(stats.shape)
        stats = merge(stats, other)
    policy_peak, reference_peak, policy_total, reference_total, weighted_sum = stats

    policy_lognorm = policy_peak + jnp.log(policy_total)
    reference_lognorm = reference_peak + jnp.log(reference_total)
    divergence = weighted_sum / policy_total - policy_lognorm + reference_lognorm
    log_ratio = difference - (policy_lognorm - reference_lognorm)[:, None]
    token_probs = jnp.exp(policy_logits - policy_lognorm[:, None])
    logit_grad = (token_probs * (log_ratio - divergence[:, None])).astype(BF16)

    got = exchange(jnp.concatenate([logit_grad[:, columns:], logit_grad[:, :columns]], 1), across_cores)
    quarter = mine // 2
    m0, m1, g0, g1 = logit_grad[:quarter], logit_grad[quarter:], got[:quarter], got[quarter:]
    by_y = jnp.stack(
        [jnp.where(second, g0, m0), jnp.where(second, m0, m1), jnp.where(second, g1, g0), jnp.where(second, m1, g1)]
    ).reshape(Y, X, Z * chip_rows, 2 * columns)
    by_y = jnp.stack(
        [
            by_y[:, 0],
            jnp.where(second, by_y[:, 2], by_y[:, 1]),
            jnp.where(second, by_y[:, 1], by_y[:, 2]),
            by_y[:, 3],
        ],
        1,
    )
    by_x = jnp.swapaxes(by_y, 0, 1).reshape(tokens, 2 * columns)
    by_y = by_y.reshape(tokens, 2 * columns)

    def share(grad, weights):
        return lax.dot_general(grad, weights, (((1,), (1,)), ((), ())), preferred_element_type=F32)

    def first_step(grad, weights, partner):
        sent = exchange(share(grad[mine:], weights).astype(BF16), partner)
        return share(grad[:mine], weights) + sent.astype(F32)

    low, high = head[: half // 2], head[half // 2 :]
    low_total = first_step(by_y, low, along_y(3, 1))
    high_total = first_step(by_x, high, along_x(3, 1))
    low_total = scatter_step(low_total, along_y(1, 3))
    high_total = scatter_step(high_total, along_x(1, 3))
    low_total = scatter_step(scatter_step(low_total, along_x(3, 1)), along_x(1, 3))
    high_total = scatter_step(scatter_step(high_total, along_y(3, 1)), along_y(1, 3))
    total = jnp.concatenate([low_total, high_total], 1)
    for step in Z_STEPS[::-1]:
        total = scatter_step(total, along_z(step))

    keep = lax.dynamic_slice_in_dim(total, c0 * own_rows, own_rows, 0)
    got = exchange(lax.dynamic_slice_in_dim(total, (1 - c0) * own_rows, own_rows, 0), across_cores)
    grad = jnp.concatenate([jnp.where(second, got, keep), jnp.where(second, keep, got)], 1)
    other_divergence = exchange(divergence[:chip_rows], across_cores)
    own_divergence = jnp.where(second, other_divergence[own_rows:chip_rows], divergence[:own_rows])
    weight = response_mask.astype(F32)
    return (weight * own_divergence, (weight[:, None] * grad).astype(BF16))


def solution(mesh):
    return jax.shard_map(
        on_device,
        mesh=mesh,
        in_specs=(
            P(("tok", "vocab"), None),
            P(("tok", "vocab"), None),
            P(None, ("tok", "vocab")),
            P(),
            P(("tok", "vocab")),
        ),
        out_specs=(P(("tok", "vocab")), P(("tok", "vocab"), None)),
        check_vma=False,
    )
```

```python
import jax
import jax.numpy as jnp
from jax import lax
from jax.sharding import Mesh, PartitionSpec as P

X, CORES, Z, Y = 4, 2, 8, 4
AXES = ("x", "core", "z", "y")
F32, BF16 = jnp.float32, jnp.bfloat16


def flat(x, c, z, y):
    return ((x * CORES + c) * Z + z) * Y + y


def exchange(value, partner):
    pairs = [
        (flat(x, c, z, y), flat(*partner(x, c, z, y)))
        for x in range(X)
        for c in range(CORES)
        for z in range(Z)
        for y in range(Y)
    ]
    return lax.ppermute(value, AXES, pairs)


def along_x(first, second):
    return lambda x, c, z, y: (x ^ (second if c else first), c, z, y)


def along_y(first, second):
    return lambda x, c, z, y: (x, c, z, y ^ (second if c else first))


def along_z(step):
    return lambda x, c, z, y: (x, c, z ^ step, y)


def across_cores(x, c, z, y):
    return (x, 1 - c, z, y)


Z_STEPS = (1, 2, 6)


def gray(j):
    return j ^ (j >> 1)


def z_slot(j):
    return j ^ ((j >> 2) << 1)


def gather_z(rows):
    for step in Z_STEPS:
        rows = jnp.concatenate([rows, exchange(rows, along_z(step))], 0)
    return rows


def ring_near(rows, along):
    return exchange(rows, along(1, 3))


def ring_far(rows, near, along):
    return exchange(jnp.concatenate([rows, near], 0), along(3, 1))


def scatter_step(total, partner):
    half = total.shape[0] // 2
    return total[:half] + exchange(total[half:].astype(BF16), partner).astype(F32)


def share(grad, weights):
    return lax.dot_general(grad, weights, (((1,), (1,)), ((), ())), preferred_element_type=F32)


def place_by(index, values):
    mask = index[:, None] == jnp.arange(values.shape[0], dtype=jnp.int32)[None]
    return jnp.sum(jnp.where(mask, values[None], 0.0), axis=1)


def on_device(policy_hidden, reference_hidden, head_weight, pair_map, response_mask):
    x0, c0, z0, y0 = (lax.axis_index(name) for name in ("x", "core", "z", "y"))
    second = c0 == 1
    swapped = (c0 ^ (y0 >> 1)) == 1
    own_rows, width = policy_hidden.shape
    half = width // 2
    part = half // 2
    columns = head_weight.shape[1]
    chip_rows = CORES * own_rows
    line = Z * chip_rows
    ring = X * line
    tokens = Y * ring
    mine = tokens // 2

    own = jnp.concatenate([policy_hidden, reference_hidden], 0)
    keep = lax.dynamic_slice_in_dim(own, c0 * half, half, 1)
    got = exchange(lax.dynamic_slice_in_dim(own, (1 - c0) * half, half, 1), across_cores)
    first_rows = jnp.where(second, got, keep)
    second_rows = jnp.where(second, keep, got)
    rows = jnp.concatenate(
        [first_rows[:own_rows], second_rows[:own_rows], first_rows[own_rows:], second_rows[own_rows:]], 0
    )
    head_keep = lax.dynamic_slice_in_dim(head_weight, c0 * half, half, 0)
    head_got = exchange(lax.dynamic_slice_in_dim(head_weight, (1 - c0) * half, half, 0), across_cores)
    head = jnp.concatenate([head_keep, head_got], 1)

    rows = gather_z(rows)
    slot = jnp.arange(tokens, dtype=jnp.int32)

    def raw(j):
        return jnp.where(second, jnp.where(j == 0, 0, jnp.where(j == 3, 1, j + 1)), gray(j))

    def unraw(k):
        return jnp.where(second, jnp.where(k == 0, 0, jnp.where(k == 1, 3, k - 1)), gray(k))

    sr, sc = slot % own_rows, (slot // own_rows) % CORES
    sz = z_slot((slot // chip_rows) % Z) ^ z0
    sx = gray((slot // line) % X) ^ x0
    half_y = slot // ring
    sy = gray(half_y ^ jnp.where(swapped, 2, 0)) ^ y0
    partner = jnp.take(pair_map, flat(sx, sc, sz, sy) * own_rows + sr, axis=0)
    rows, head, partner = lax.optimization_barrier((rows, head, partner))
    pr, pdev = partner % own_rows, partner // own_rows
    py, pz, pc, px = pdev % Y, (pdev // Y) % Z, (pdev // (Y * Z)) % CORES, pdev // (Y * Z * CORES)

    rows = rows.reshape(Z, 2, chip_rows, half).swapaxes(0, 1).reshape(2 * line, half)
    low, high = rows[:, :part], rows[:, part:]
    low_near, high_near = ring_near(low, along_x), ring_near(high, along_y)
    low_far, high_far = ring_far(low, low_near, along_x), ring_far(high, high_near, along_y)

    def order(rows, near, far, start):
        count = 2 * line
        far0, far1 = far[:count], far[count:]
        blocks = [rows, jnp.where(second, far0, near), jnp.where(second, near, far0), far1]
        return jnp.concatenate([block[start : start + line] for block in blocks], 0)

    gathered = []
    for start in (line, 0):
        a = order(low, low_near, low_far, start)
        b = order(high, high_near, high_far, start)
        a_near, b_near = ring_near(a, along_y), ring_near(b, along_x)
        gathered.append((a, a_near, b, b_near))
    (ra, ra_near, rb, rb_near), (pa, pa_near, pb, pb_near) = gathered
    ra_far, rb_far = ring_far(ra, ra_near, along_y), ring_far(rb, rb_near, along_x)
    pa_far, pb_far = ring_far(pa, pa_near, along_y), ring_far(pb, pb_near, along_x)

    tail = (z_slot(pz ^ z0) * CORES + pc) * own_rows + pr
    low_place = (raw(py ^ y0) * X + gray(px ^ x0)) * line + tail
    high_place = (raw(px ^ x0) * Y + gray(py ^ y0)) * line + tail
    head_low, head_high = head[:part], head[part:]

    def pick(place, blocks):
        one_hot = (place[:, None] == jnp.arange(tokens, dtype=jnp.int32)[None]).astype(BF16)
        return jnp.dot(one_hot, jnp.concatenate(blocks, 0), preferred_element_type=F32).astype(BF16)

    def product(a, b):
        return jnp.dot(a, head_low, preferred_element_type=F32) + jnp.dot(b, head_high, preferred_element_type=F32)

    reference_part = product(pick(low_place, (ra, ra_near, ra_far)), pick(high_place, (rb, rb_near, rb_far)))

    def swap_columns(v):
        return jnp.concatenate([v[:, columns:], v[:, :columns]], 1)

    reference_logits = reference_part[:mine] + swap_columns(exchange(reference_part[mine:], across_cores))

    def policy_blocks():
        low_y = [pa, jnp.where(second, pa_far[:ring], pa_near), jnp.where(second, pa_near, pa_far[:ring]), pa_far[ring:]]
        high_x = [pb, jnp.where(second, pb_far[:ring], pb_near), jnp.where(second, pb_near, pb_far[:ring]), pb_far[ring:]]
        out_low, out_high = [], []
        for y in range(Y):
            out_low.append(low_y[y])
            out_high.append(jnp.concatenate([block[y * line : (y + 1) * line] for block in high_x], 0))
        return jnp.concatenate(out_low, 0), jnp.concatenate(out_high, 0)

    policy_low, policy_high = policy_blocks()
    policy_part = product(policy_low, policy_high)
    policy_keep = jnp.where(swapped, policy_part[mine:], policy_part[:mine])
    policy_send = jnp.where(swapped, policy_part[:mine], policy_part[mine:])
    policy_logits = policy_keep + swap_columns(exchange(policy_send, across_cores))
    difference = policy_logits - reference_logits

    policy_peak = jnp.max(policy_logits, axis=1)
    reference_peak = jnp.max(reference_logits, axis=1)
    policy_exp = jnp.exp(policy_logits - policy_peak[:, None])
    reference_exp = jnp.exp(reference_logits - reference_peak[:, None])
    policy_total = jnp.sum(policy_exp, axis=1)
    policy_lse = policy_peak + jnp.log(policy_total)
    reference_lse = reference_peak + jnp.log(jnp.sum(reference_exp, axis=1))
    center = jnp.sum(policy_exp * difference, axis=1) / policy_total

    common = ((sy * X + sx) * Z + sz) * chip_rows + sc * own_rows + sr
    in_common = jnp.arange(mine, dtype=jnp.int32) + c0 * mine
    match = common[None, :mine] == in_common[:, None]

    def to_common(v):
        return jnp.sum(jnp.where(match, v[None], 0.0), axis=1)

    local = jnp.stack([to_common(policy_lse), to_common(reference_lse), to_common(center)])
    peak_common = to_common(policy_peak)
    chips = X * Y * Z
    message = jnp.concatenate([local, jnp.zeros((1, mine), F32)]).reshape(8, mine // 2)
    everyone = lax.all_to_all(jnp.broadcast_to(message[None], (chips,) + message.shape), ("x", "z", "y"), 0, 0)
    everyone = everyone.reshape(chips, 4, mine)

    grad = jnp.concatenate([(policy_exp * (difference - center[:, None])).astype(BF16), policy_exp.astype(BF16)], 0)
    got = exchange(swap_columns(grad), across_cores)
    grad, got = grad.reshape(2, 2, ring, 2 * columns), got.reshape(2, 2, ring, 2 * columns)
    r0 = jnp.where(swapped, got[:, 0], grad[:, 0])
    r1 = jnp.where(swapped, got[:, 1], grad[:, 1])
    r3 = jnp.where(swapped, grad[:, 0], got[:, 0])
    r2 = jnp.where(swapped, grad[:, 1], got[:, 1])
    by_y = jnp.stack([r0, jnp.where(second, r3, r1), jnp.where(second, r1, r3), r2], 1)
    by_y = by_y.reshape(2, Y, X, line, 2 * columns)
    by_y = jnp.stack(
        [
            by_y[:, :, 0],
            jnp.where(second, by_y[:, :, 2], by_y[:, :, 1]),
            jnp.where(second, by_y[:, :, 1], by_y[:, :, 2]),
            by_y[:, :, 3],
        ],
        2,
    )
    by_x = jnp.swapaxes(by_y, 1, 2).reshape(2 * tokens, 2 * columns)
    by_y = by_y.reshape(2 * tokens, 2 * columns)
    low_sums = share(by_y, head_low)
    high_sums = share(by_x, head_high)

    policy_all = jnp.max(everyone[:, 0], axis=0)
    reference_all = jnp.max(everyone[:, 1], axis=0)
    policy_weights = jnp.exp(everyone[:, 0] - policy_all)
    total = jnp.sum(policy_weights, axis=0)
    policy_lognorm = policy_all + jnp.log(total)
    reference_lognorm = reference_all + jnp.log(jnp.sum(jnp.exp(everyone[:, 1] - reference_all), axis=0))
    mean = jnp.sum(policy_weights * everyone[:, 2], axis=0) / total
    divergence = mean - policy_lognorm + reference_lognorm
    scale = jnp.exp(peak_common - policy_lognorm)
    shift = scale * (local[2] - mean)
    result = jnp.stack([scale, shift, divergence])
    other = exchange(result, across_cores)
    scale, shift, divergence = jnp.concatenate(
        [jnp.where(second, other, result), jnp.where(second, result, other)], 1
    )

    outer, inner = unraw(slot // ring), unraw((slot // line) % X)
    y_index = (((outer ^ y0) * X + (inner ^ x0)) * Z + sz) * chip_rows + slot % chip_rows
    x_index = (((inner ^ y0) * X + (outer ^ x0)) * Z + sz) * chip_rows + slot % chip_rows

    def scaled(sums, index, start):
        rows_scale = place_by(index[start : start + mine], scale)
        rows_shift = place_by(index[start : start + mine], shift)
        return rows_scale[:, None] * sums[start : start + mine] + rows_shift[:, None] * sums[tokens + start : tokens + start + mine]

    def first_step(sums, index, partner):
        sent = exchange(scaled(sums, index, mine).astype(BF16), partner)
        return scaled(sums, index, 0) + sent.astype(F32)

    low_total = first_step(low_sums, y_index, along_y(3, 1))
    high_total = first_step(high_sums, x_index, along_x(3, 1))
    low_total = scatter_step(low_total, along_y(1, 3))
    high_total = scatter_step(high_total, along_x(1, 3))
    low_total = scatter_step(scatter_step(low_total, along_x(3, 1)), along_x(1, 3))
    high_total = scatter_step(scatter_step(high_total, along_y(3, 1)), along_y(1, 3))
    total = jnp.concatenate([low_total, high_total], 1)
    for step in Z_STEPS[::-1]:
        total = scatter_step(total, along_z(step))

    keep = lax.dynamic_slice_in_dim(total, c0 * own_rows, own_rows, 0)
    got = exchange(lax.dynamic_slice_in_dim(total, (1 - c0) * own_rows, own_rows, 0), across_cores)
    grad = jnp.concatenate([jnp.where(second, got, keep), jnp.where(second, keep, got)], 1)
    position = ((y0 * X + x0) * Z + z0) * chip_rows + c0 * own_rows
    own_divergence = lax.dynamic_slice_in_dim(divergence, position, own_rows, 0)
    weight = response_mask.astype(F32)
    return (weight * own_divergence, (weight[:, None] * grad).astype(BF16))


def solution(mesh):
    chips = Mesh(mesh.devices.reshape(X, CORES, Z, Y), AXES)
    return jax.shard_map(
        on_device,
        mesh=chips,
        in_specs=(P(AXES, None), P(AXES, None), P(None, AXES), P(), P(AXES)),
        out_specs=(P(AXES), P(AXES, None)),
        check_vma=False,
    )
```

```python
import functools

import jax
import jax.numpy as jnp
from jax import lax
from jax.experimental import pallas as pl
from jax.experimental.pallas import tpu as pltpu
from jax.sharding import Mesh, PartitionSpec as P

X, CORES, Z, Y = 4, 2, 8, 4
AXES = ("x", "core", "z", "y")
F32, BF16 = jnp.float32, jnp.bfloat16


def flat(x, c, z, y):
    return ((x * CORES + c) * Z + z) * Y + y


def exchange(value, partner):
    pairs = [
        (flat(x, c, z, y), flat(*partner(x, c, z, y)))
        for x in range(X)
        for c in range(CORES)
        for z in range(Z)
        for y in range(Y)
    ]
    return lax.ppermute(value, AXES, pairs)


def along_x(first, second):
    return lambda x, c, z, y: (x ^ (second if c else first), c, z, y)


def along_y(first, second):
    return lambda x, c, z, y: (x, c, z, y ^ (second if c else first))


def along_z(step):
    return lambda x, c, z, y: (x, c, z ^ step, y)


def across_cores(x, c, z, y):
    return (x, 1 - c, z, y)


Z_STEPS = (1, 2, 6)


def gray(j):
    return j ^ (j >> 1)


def z_slot(j):
    return j ^ ((j >> 2) << 1)


def gather_z(rows):
    for step in Z_STEPS:
        rows = jnp.concatenate([rows, exchange(rows, along_z(step))], 0)
    return rows


def ring_near(rows, along):
    return exchange(rows, along(1, 3))


def ring_far(rows, near, along):
    return exchange(jnp.concatenate([rows, near], 0), along(3, 1))


def scatter_step(total, partner):
    half = total.shape[0] // 2
    return total[:half] + exchange(total[half:].astype(BF16), partner).astype(F32)


CONTRACT_LAST = (((1,), (1,)), ((), ()))
VMEM_LIMIT = 40 * 1024 * 1024


def whole(array):
    zeros = (0,) * array.ndim
    return pl.BlockSpec(array.shape, lambda *_: zeros)


def run(kernel, name, flags, operands, outputs, grid=(1,), scratch=(), in_specs=None, out_specs=None, flops=0):
    bytes_accessed = sum(v.size * v.dtype.itemsize for v in (*operands, *outputs))
    return pl.pallas_call(
        kernel,
        out_shape=outputs,
        grid_spec=pltpu.PrefetchScalarGridSpec(
            num_scalar_prefetch=1,
            grid=grid,
            in_specs=in_specs or [whole(v) for v in operands],
            out_specs=out_specs or [whole(v) for v in outputs],
            scratch_shapes=list(scratch),
        ),
        compiler_params=pltpu.CompilerParams(vmem_limit_bytes=VMEM_LIMIT),
        cost_estimate=pl.CostEstimate(flops=flops, bytes_accessed=bytes_accessed, transcendentals=0),
        name=name,
    )(flags, *operands)


def ring_places(core):
    return (0, 1 + core, 2 - core, 3)


def rows_at(block, count):
    return pl.ds(pl.multiple_of(block * count, count), count)


def order_kernel(line, flags, low, low_near, low_far, high, high_near, high_far, ra, rb, pa, pb):
    places = ring_places(flags[0])
    for rows, near, far, base, policy in ((low, low_near, low_far, ra, pa), (high, high_near, high_far, rb, pb)):
        count = 2 * line
        pieces = ((rows, 0), (near, 0), (far, 0), (far, count))
        for (piece, start), place in zip(pieces, places):
            policy[rows_at(place, line), :] = piece[start : start + line, :]
            base[rows_at(place, line), :] = piece[start + line : start + count, :]


def two_products(x, part, head_keep, head_got):
    def product(head):
        return jnp.dot(x[0], head[:part, :], preferred_element_type=F32) + jnp.dot(
            x[1], head[part:, :], preferred_element_type=F32
        )

    return product(head_keep), product(head_got)


def store_halves(own, other, keep, send):
    columns = own.shape[1]
    step = pl.program_id(0)

    @pl.when(step == 0)
    def _():
        keep[:, :columns] = own
        keep[:, columns:] = other

    @pl.when(step == 1)
    def _():
        send[:, :columns] = other
        send[:, columns:] = own


def base_kernel(
    flags, low_place, high_place, a, a_near, a_far, b, b_near, b_far, head_keep, head_got, keep, send
):
    def pick(place, rows, near, far):
        count, ring = place.shape[0], rows.shape[0]
        lanes = lax.broadcasted_iota(jnp.int32, (count, 4 * ring), 1)
        one_hot = jnp.where(place[...] == lanes, 1.0, 0.0).astype(BF16)
        total = jnp.dot(one_hot[:, :ring], rows[...], preferred_element_type=F32)
        total += jnp.dot(one_hot[:, ring : 2 * ring], near[...], preferred_element_type=F32)
        total += jnp.dot(one_hot[:, 2 * ring :], far[...], preferred_element_type=F32)
        return total.astype(BF16)

    x = (pick(low_place, a, a_near, a_far), pick(high_place, b, b_near, b_far))
    own, other = two_products(x, a.shape[1], head_keep, head_got)
    store_halves(own, other, keep, send)


def policy_kernel(line, flags, a, a_near, a_far, b, b_near, b_far, head_keep, head_got, keep, send, rows):
    step = pl.program_id(0)
    ring, part = a.shape
    mine = keep.shape[0]

    @pl.when(step == 0)
    def _():
        places = ring_places(flags[0])
        flip = 2 * flags[1]
        low = (a[...], a_near[...], a_far[:ring, :], a_far[ring:, :])
        for piece, place in zip(low, places):
            rows[rows_at(place ^ flip, ring), :part] = piece
        high = ((b, 0), (b_near, 0), (b_far, 0), (b_far, ring))
        for (piece, start), place in zip(high, places):
            for y in range(Y):
                rows[rows_at((y ^ flip) * X + place, line), part:] = piece[start + y * line : start + (y + 1) * line, :]

    x = rows[rows_at(step, mine), :]
    own, other = two_products((x[:, :part], x[:, part:]), part, head_keep, head_got)
    store_halves(own, other, keep, send)


def local_kernel(flags, common, policy_keep, policy_got, base_keep, base_got, message, parts, parts_sent):
    step = pl.program_id(0)
    policy = policy_keep[...] + policy_got[...]
    base = base_keep[...] + base_got[...]
    difference = policy - base
    columns = policy.shape[1] // 2
    policy_peak = jnp.max(policy, axis=1, keepdims=True)
    base_peak = jnp.max(base, axis=1, keepdims=True)
    policy_exp = jnp.exp(policy - policy_peak)
    policy_total = jnp.sum(policy_exp, axis=1, keepdims=True)
    base_total = jnp.sum(jnp.exp(base - base_peak), axis=1, keepdims=True)
    center = jnp.sum(policy_exp * difference, axis=1, keepdims=True) / policy_total
    first = (policy_exp * (difference - center)).astype(BF16)
    second = policy_exp.astype(BF16)
    for i, v in enumerate((first, second)):
        parts[i] = v
        parts_sent[i, :, :columns] = v[:, columns:]
        parts_sent[i, :, columns:] = v[:, :columns]
    mine = message.shape[1]
    lanes = lax.broadcasted_iota(jnp.int32, (policy.shape[0], mine), 1) + flags[0] * mine
    match = common[...] == lanes
    values = (
        policy_peak + jnp.log(policy_total),
        base_peak + jnp.log(base_total),
        center,
        policy_peak,
    )
    lines = [jnp.sum(jnp.where(match, v, 0.0), axis=0, keepdims=True) for v in values]
    block = jnp.concatenate(lines + [jnp.zeros((4, mine), F32)], axis=0)

    @pl.when(step == 0)
    def _():
        message[...] = block

    @pl.when(step > 0)
    def _():
        message[...] += block


def merged(messages):
    policy, base, mean = messages[:, 0], messages[:, 1], messages[:, 2]
    policy_peak = jnp.max(policy, axis=0, keepdims=True)
    base_peak = jnp.max(base, axis=0, keepdims=True)
    weights = jnp.exp(policy - policy_peak)
    total = jnp.sum(weights, axis=0, keepdims=True)
    base_total = jnp.sum(jnp.exp(base - base_peak), axis=0, keepdims=True)
    return (
        policy_peak + jnp.log(total),
        base_peak + jnp.log(base_total),
        jnp.sum(weights * mean, axis=0, keepdims=True) / total,
    )


def merge_kernel(flags, messages, out):
    lines = merged(messages[...])
    out[...] = jnp.concatenate([*lines, jnp.zeros((5, out.shape[1]), F32)], axis=0)


def result_kernel(flags, messages, local, out):
    policy, base, mean = merged(messages[...])
    scale = jnp.exp(local[3:4, :] - policy)
    out[...] = jnp.concatenate(
        [scale, local[2:3, :] - mean, mean - policy + base, jnp.zeros((5, out.shape[1]), F32)], axis=0
    )


def sent_kernel(
    line, flags, common, result, result_got, parts, parts_got, head_keep, head_got, low, high, low_rows, high_rows, by_y, by_x
):
    mine = result.shape[1]
    core, flip = flags[0], 2 * flags[1]

    def raw(place):
        return jnp.where((place == 1) | (place == 2), jnp.where(core == 1, 3 - place, place), place)

    for h, (values, source) in enumerate(((result, parts), (result_got, parts_got))):
        first = (core if h == 0 else 1 - core) * mine
        lanes = lax.broadcasted_iota(jnp.int32, (mine, mine), 1) + first
        match = common[h * mine : (h + 1) * mine, :] == lanes
        scale = jnp.sum(jnp.where(match, values[0:1, :], 0.0), axis=1, keepdims=True)
        shift = jnp.sum(jnp.where(match, values[1:2, :], 0.0), axis=1, keepdims=True)
        grad = (scale * (source[0].astype(F32) + shift * source[1].astype(F32))).astype(BF16)
        for block in range(2 * X):
            y, x = raw((2 * h + block // X) ^ flip), raw(block % X + 0 * core)
            piece = grad[block * line : (block + 1) * line]
            by_y[rows_at(y * X + x, line), :] = piece
            by_x[rows_at(x * Y + y, line), :] = piece
    low[...] = gradient(by_y[mine:, :], head_keep, head_got, 0).astype(BF16)
    high[...] = gradient(by_x[mine:, :], head_keep, head_got, 1).astype(BF16)
    low_rows[...] = by_y[:mine, :]
    high_rows[...] = by_x[:mine, :]


def gradient(rows, head_keep, head_got, which):
    columns = head_keep.shape[1]
    part = head_keep.shape[0] // 2
    span = slice(which * part, (which + 1) * part)
    return lax.dot_general(
        rows[:, :columns], head_keep[span, :], CONTRACT_LAST, preferred_element_type=F32
    ) + lax.dot_general(rows[:, columns:], head_got[span, :], CONTRACT_LAST, preferred_element_type=F32)


def kept_kernel(flags, low_rows, high_rows, head_keep, head_got, low, high):
    low[...] = gradient(low_rows[...], head_keep, head_got, 0)
    high[...] = gradient(high_rows[...], head_keep, head_got, 1)


def on_device(policy_hidden, reference_hidden, head_weight, pair_map, response_mask):
    x0, c0, z0, y0 = (lax.axis_index(name) for name in ("x", "core", "z", "y"))
    second = c0 == 1
    swapped = (c0 ^ (y0 >> 1)) == 1
    own_rows, width = policy_hidden.shape
    half = width // 2
    part = half // 2
    columns = head_weight.shape[1]
    chip_rows = CORES * own_rows
    line = Z * chip_rows
    ring = X * line
    tokens = Y * ring
    mine = tokens // 2

    own = jnp.concatenate([policy_hidden, reference_hidden], 0)
    keep = lax.dynamic_slice_in_dim(own, c0 * half, half, 1)
    got = exchange(lax.dynamic_slice_in_dim(own, (1 - c0) * half, half, 1), across_cores)
    first_rows = jnp.where(second, got, keep)
    second_rows = jnp.where(second, keep, got)
    rows = jnp.concatenate(
        [first_rows[:own_rows], second_rows[:own_rows], first_rows[own_rows:], second_rows[own_rows:]], 0
    )
    rows, head_weight = lax.optimization_barrier((rows, head_weight))
    head_got = exchange(lax.dynamic_slice_in_dim(head_weight, (1 - c0) * half, half, 0), across_cores)
    flags = jnp.stack([c0, c0 ^ (y0 >> 1)]).astype(jnp.int32)
    head = (head_weight, head_got)
    head_specs = [pl.BlockSpec((half, columns), lambda i, f: (f[0], 0)), whole(head_got)]

    rows = gather_z(rows)

    slot = jnp.arange(tokens, dtype=jnp.int32)

    def raw(j):
        return jnp.where(second, jnp.where(j == 0, 0, jnp.where(j == 3, 1, j + 1)), gray(j))

    sr, sc = slot % own_rows, (slot // own_rows) % CORES
    sz = z_slot((slot // chip_rows) % Z) ^ z0
    sx = gray((slot // line) % X) ^ x0
    sy = gray((slot // ring) ^ jnp.where(swapped, 2, 0)) ^ y0
    partner = jnp.take(pair_map, flat(sx, sc, sz, sy) * own_rows + sr, axis=0)
    pr, pdev = partner % own_rows, partner // own_rows
    py, pz, pc, px = pdev % Y, (pdev // Y) % Z, (pdev // (Y * Z)) % CORES, pdev // (Y * Z * CORES)
    tail = (z_slot(pz ^ z0) * CORES + pc) * own_rows + pr
    low_place = ((raw(py ^ y0) * X + gray(px ^ x0)) * line + tail)[:, None]
    high_place = ((raw(px ^ x0) * Y + gray(py ^ y0)) * line + tail)[:, None]
    common = (((sy * X + sx) * Z + sz) * chip_rows + sc * own_rows + sr)[:, None]

    rows = rows.reshape(Z, 2, chip_rows, half).swapaxes(0, 1).reshape(2 * line, half)
    low, high = rows[:, :part], rows[:, part:]
    low_near, high_near = ring_near(low, along_x), ring_near(high, along_y)
    low_far, high_far = ring_far(low, low_near, along_x), ring_far(high, high_near, along_y)
    block = jax.ShapeDtypeStruct((ring, part), BF16)
    ra, rb, pa, pb = run(
        functools.partial(order_kernel, line),
        "order",
        flags,
        (low, low_near, low_far, high, high_near, high_far),
        [block] * 4,
    )

    ra_near, rb_near = ring_near(ra, along_y), ring_near(rb, along_x)
    pa_near, pb_near = ring_near(pa, along_y), ring_near(pb, along_x)
    ra_far, rb_far = ring_far(ra, ra_near, along_y), ring_far(rb, rb_near, along_x)
    pa_far, pb_far = ring_far(pa, pa_near, along_y), ring_far(pb, pb_near, along_x)

    logits = [jax.ShapeDtypeStruct((mine, 2 * columns), F32)] * 2
    flops = 4 * tokens * half * columns
    base = (ra, ra_near, ra_far, rb, rb_near, rb_far)
    base_keep, base_send = run(
        base_kernel,
        "base_logits",
        flags,
        (low_place, high_place, *base, *head),
        logits,
        grid=(2,),
        in_specs=[pl.BlockSpec((mine, 1), lambda i, f: (i, 0))] * 2 + [whole(v) for v in base] + head_specs,
        flops=2 * flops,
    )
    base_got = exchange(base_send, across_cores)
    policy = (pa, pa_near, pa_far, pb, pb_near, pb_far)
    policy_keep, policy_send = run(
        functools.partial(policy_kernel, line),
        "policy_logits",
        flags,
        (*policy, *head),
        logits,
        grid=(2,),
        in_specs=[whole(v) for v in policy] + head_specs,
        scratch=[pltpu.VMEM((tokens, half), BF16)],
        flops=flops,
    )
    policy_got = exchange(policy_send, across_cores)

    steps = 4
    row_spec = pl.BlockSpec((mine // steps, 2 * columns), lambda i, f: (i, 0))
    part_spec = pl.BlockSpec((2, mine // steps, 2 * columns), lambda i, f: (0, i, 0))
    message_shape = jax.ShapeDtypeStruct((8, mine), F32)
    parts_shape = jax.ShapeDtypeStruct((2, mine, 2 * columns), BF16)
    message, parts, parts_sent = run(
        local_kernel,
        "local_sums",
        flags,
        (common[:mine], policy_keep, policy_got, base_keep, base_got),
        [message_shape, parts_shape, parts_shape],
        grid=(steps,),
        in_specs=[pl.BlockSpec((mine // steps, 1), lambda i, f: (i, 0))] + [row_spec] * 4,
        out_specs=[whole(message_shape), part_spec, part_spec],
    )
    parts_got = exchange(parts_sent, across_cores)

    gathered = message
    for step in Z_STEPS:
        gathered = jnp.concatenate([gathered, exchange(gathered, along_z(step))], 0)
    (line_message,) = run(merge_kernel, "merge", flags, (gathered.reshape(Z, 8, mine),), [message_shape])
    everyone = lax.all_to_all(jnp.broadcast_to(line_message[None], (X * Y, 8, mine)), ("x", "y"), 0, 0)
    (result,) = run(result_kernel, "result", flags, (everyone, message), [message_shape])
    result_got = exchange(result, across_cores)

    rows_shape = jax.ShapeDtypeStruct((mine, 2 * columns), BF16)
    sent_shape = jax.ShapeDtypeStruct((mine, part), BF16)
    kept_shape = jax.ShapeDtypeStruct((mine, part), F32)
    operands = (common, result, result_got, parts, parts_got)
    low_sent, high_sent, low_rows, high_rows = run(
        functools.partial(sent_kernel, line),
        "gradient_sent",
        flags,
        (*operands, *head),
        [sent_shape, sent_shape, rows_shape, rows_shape],
        in_specs=[whole(v) for v in operands] + head_specs,
        scratch=[pltpu.VMEM((tokens, 2 * columns), BF16)] * 2,
        flops=flops // 2,
    )
    low_got, high_got = exchange(low_sent, along_y(3, 1)), exchange(high_sent, along_x(3, 1))
    low_kept, high_kept = run(
        kept_kernel,
        "gradient_kept",
        flags,
        (low_rows, high_rows, *head),
        [kept_shape, kept_shape],
        in_specs=[whole(low_rows), whole(high_rows)] + head_specs,
        flops=flops // 2,
    )
    low_total = low_kept + low_got.astype(F32)
    high_total = high_kept + high_got.astype(F32)
    low_total = scatter_step(low_total, along_y(1, 3))
    high_total = scatter_step(high_total, along_x(1, 3))
    low_total = scatter_step(scatter_step(low_total, along_x(3, 1)), along_x(1, 3))
    high_total = scatter_step(scatter_step(high_total, along_y(3, 1)), along_y(1, 3))
    total = jnp.concatenate([low_total, high_total], 1)
    for step in Z_STEPS[::-1]:
        total = scatter_step(total, along_z(step))

    keep = lax.dynamic_slice_in_dim(total, c0 * own_rows, own_rows, 0)
    got = exchange(lax.dynamic_slice_in_dim(total, (1 - c0) * own_rows, own_rows, 0), across_cores)
    grad = jnp.concatenate([jnp.where(second, got, keep), jnp.where(second, keep, got)], 1)
    position = ((y0 * X + x0) * Z + z0) * chip_rows + c0 * own_rows
    divergence = jnp.where(second, jnp.stack([result_got[2], result[2]]), jnp.stack([result[2], result_got[2]]))
    own_divergence = lax.dynamic_slice_in_dim(divergence.reshape(-1), position, own_rows, 0)
    weight = response_mask.astype(F32)
    return (weight * own_divergence, (weight[:, None] * grad).astype(BF16))


def solution(mesh):
    chips = Mesh(mesh.devices.reshape(X, CORES, Z, Y), AXES)
    return jax.shard_map(
        on_device,
        mesh=chips,
        in_specs=(P(AXES, None), P(AXES, None), P(None, AXES), P(), P(AXES)),
        out_specs=(P(AXES), P(AXES, None)),
        check_vma=False,
    )
```

```python
import functools

import jax
import jax.numpy as jnp
from jax import lax
from jax.experimental import pallas as pl
from jax.experimental.pallas import tpu as pltpu
from jax.sharding import Mesh, PartitionSpec as P

X, CORES, Z, Y = 4, 2, 8, 4
AXES = ("x", "core", "z", "y")
F32, BF16 = jnp.float32, jnp.bfloat16


def flat(x, c, z, y):
    return ((x * CORES + c) * Z + z) * Y + y


def exchange(value, partner):
    pairs = [
        (flat(x, c, z, y), flat(*partner(x, c, z, y)))
        for x in range(X)
        for c in range(CORES)
        for z in range(Z)
        for y in range(Y)
    ]
    return lax.ppermute(value, AXES, pairs)


def along_x(first, second):
    return lambda x, c, z, y: (x ^ (second if c else first), c, z, y)


def along_y(first, second):
    return lambda x, c, z, y: (x, c, z, y ^ (second if c else first))


def along_z(step):
    return lambda x, c, z, y: (x, c, z ^ step, y)


def across_cores(x, c, z, y):
    return (x, 1 - c, z, y)


Z_STEPS = (1, 2, 6)


def gray(j):
    return j ^ (j >> 1)


def z_slot(j):
    return j ^ ((j >> 2) << 1)


def gather_z(rows):
    for step in Z_STEPS:
        rows = jnp.concatenate([rows, exchange(rows, along_z(step))], 0)
    return rows


def ring_near(rows, along):
    return exchange(rows, along(1, 3))


def ring_far(rows, near, along):
    return exchange(jnp.concatenate([rows, near], 0), along(3, 1))


def scatter_step(total, partner):
    half = total.shape[0] // 2
    return total[:half] + exchange(total[half:].astype(BF16), partner).astype(F32)


CONTRACT_LAST = (((1,), (1,)), ((), ()))
VMEM_LIMIT = 24 * 1024 * 1024


WHOLE = pl.BlockSpec(memory_space=pltpu.VMEM)


def run(kernel, name, flags, operands, outputs, grid=(1,), scratch=(), in_specs=None, flops=0):
    bytes_accessed = sum(v.size * v.dtype.itemsize for v in (*operands, *outputs))
    return pl.pallas_call(
        kernel,
        out_shape=outputs,
        grid_spec=pltpu.PrefetchScalarGridSpec(
            num_scalar_prefetch=1,
            grid=grid,
            in_specs=in_specs or [WHOLE] * len(operands),
            out_specs=[WHOLE] * len(outputs),
            scratch_shapes=list(scratch),
        ),
        compiler_params=pltpu.CompilerParams(vmem_limit_bytes=VMEM_LIMIT),
        cost_estimate=pl.CostEstimate(flops=flops, bytes_accessed=bytes_accessed, transcendentals=0),
        name=name,
    )(flags, *operands)


def ring_places(core):
    return (0, 1 + core, 2 - core, 3)


def rows_at(block, count):
    return pl.ds(pl.multiple_of(block * count, count), count)


def order_kernel(line, flags, low, low_near, low_far, high, high_near, high_far, ra, rb, pa, pb):
    places = ring_places(flags[0])
    for rows, near, far, base, policy in ((low, low_near, low_far, ra, pa), (high, high_near, high_far, rb, pb)):
        count = 2 * line
        pieces = ((rows, 0), (near, 0), (far, 0), (far, count))
        for (piece, start), place in zip(pieces, places):
            policy[rows_at(place, line), :] = piece[start : start + line, :]
            base[rows_at(place, line), :] = piece[start + line : start + count, :]


def take_head(flags, head, head_keep):
    head_keep[...] = head[...]


def two_products(core, x, part, head_keep, head_got):
    def product(head, first):
        return jnp.dot(x[0], head[first(0), :], preferred_element_type=F32) + jnp.dot(
            x[1], head[first(1), :], preferred_element_type=F32
        )

    own = product(head_keep, lambda i: pl.ds(i * part, part))
    return own, product(head_got, lambda i: pl.ds(pl.multiple_of(core * 2 * part + i * part, part), part))


def store_halves(own, other, keep, send):
    columns = own.shape[1]
    step = pl.program_id(0)

    @pl.when(step == 0)
    def _():
        keep[:, :columns] = own
        keep[:, columns:] = other

    @pl.when(step == 1)
    def _():
        send[:, :columns] = other
        send[:, columns:] = own


def base_kernel(
    flags, low_place, high_place, a, a_near, a_far, b, b_near, b_far, head_keep, head_got, keep, send
):
    count = keep.shape[0]
    here = rows_at(pl.program_id(0), count)

    def pick(place, rows, near, far):
        ring = rows.shape[0]
        lanes = lax.broadcasted_iota(jnp.int32, (count, 4 * ring), 1)
        one_hot = jnp.where(place[here, :] == lanes, 1.0, 0.0).astype(BF16)
        total = jnp.dot(one_hot[:, :ring], rows[...], preferred_element_type=F32)
        total += jnp.dot(one_hot[:, ring : 2 * ring], near[...], preferred_element_type=F32)
        total += jnp.dot(one_hot[:, 2 * ring :], far[...], preferred_element_type=F32)
        return total.astype(BF16)

    x = (pick(low_place, a, a_near, a_far), pick(high_place, b, b_near, b_far))
    own, other = two_products(flags[0], x, a.shape[1], head_keep, head_got)
    store_halves(own, other, keep, send)


def policy_kernel(line, flags, a, a_near, a_far, b, b_near, b_far, head_keep, head_got, keep, send, rows):
    step = pl.program_id(0)
    ring, part = a.shape
    mine = keep.shape[0]

    @pl.when(step == 0)
    def _():
        places = ring_places(flags[0])
        flip = 2 * flags[1]
        low = (a[...], a_near[...], a_far[:ring, :], a_far[ring:, :])
        for piece, place in zip(low, places):
            rows[rows_at(place ^ flip, ring), :part] = piece
        high = ((b, 0), (b_near, 0), (b_far, 0), (b_far, ring))
        for (piece, start), place in zip(high, places):
            for y in range(Y):
                rows[rows_at((y ^ flip) * X + place, line), part:] = piece[start + y * line : start + (y + 1) * line, :]

    x = rows[rows_at(step, mine), :]
    own, other = two_products(flags[0], (x[:, :part], x[:, part:]), part, head_keep, head_got)
    store_halves(own, other, keep, send)


def local_kernel(steps, flags, common, policy_keep, policy_got, base_keep, base_got, message, parts, parts_sent):
    step = pl.program_id(0)
    here = rows_at(step, policy_keep.shape[0] // steps)
    policy = policy_keep[here, :] + policy_got[here, :]
    base = base_keep[here, :] + base_got[here, :]
    difference = policy - base
    columns = policy.shape[1] // 2
    policy_peak = jnp.max(policy, axis=1, keepdims=True)
    base_peak = jnp.max(base, axis=1, keepdims=True)
    policy_exp = jnp.exp(policy - policy_peak)
    policy_total = jnp.sum(policy_exp, axis=1, keepdims=True)
    base_total = jnp.sum(jnp.exp(base - base_peak), axis=1, keepdims=True)
    center = jnp.sum(policy_exp * difference, axis=1, keepdims=True) / policy_total
    first = (policy_exp * (difference - center)).astype(BF16)
    second = policy_exp.astype(BF16)
    for i, v in enumerate((first, second)):
        parts[i, here, :] = v
        parts_sent[i, here, :columns] = v[:, columns:]
        parts_sent[i, here, columns:] = v[:, :columns]
    mine = message.shape[1]
    lanes = lax.broadcasted_iota(jnp.int32, (policy.shape[0], mine), 1) + flags[0] * mine
    match = common[here, :] == lanes
    values = (
        policy_peak + jnp.log(policy_total),
        base_peak + jnp.log(base_total),
        center,
        policy_peak,
    )
    lines = [jnp.sum(jnp.where(match, v, 0.0), axis=0, keepdims=True) for v in values]
    block = jnp.concatenate(lines + [jnp.zeros((4, mine), F32)], axis=0)

    @pl.when(step == 0)
    def _():
        message[...] = block

    @pl.when(step > 0)
    def _():
        message[...] += block


def merged(messages):
    policy, base, mean = messages[:, 0], messages[:, 1], messages[:, 2]
    policy_peak = jnp.max(policy, axis=0, keepdims=True)
    base_peak = jnp.max(base, axis=0, keepdims=True)
    weights = jnp.exp(policy - policy_peak)
    total = jnp.sum(weights, axis=0, keepdims=True)
    base_total = jnp.sum(jnp.exp(base - base_peak), axis=0, keepdims=True)
    return (
        policy_peak + jnp.log(total),
        base_peak + jnp.log(base_total),
        jnp.sum(weights * mean, axis=0, keepdims=True) / total,
    )


def merge_kernel(flags, messages, out):
    lines = merged(messages[...])
    out[...] = jnp.concatenate([*lines, jnp.zeros((5, out.shape[1]), F32)], axis=0)


def result_kernel(flags, messages, local, out):
    policy, base, mean = merged(messages[...])
    scale = jnp.exp(local[3:4, :] - policy)
    out[...] = jnp.concatenate(
        [scale, local[2:3, :] - mean, mean - policy + base, jnp.zeros((5, out.shape[1]), F32)], axis=0
    )


def sent_kernel(
    line, flags, common, result, result_got, parts, parts_got, head_keep, head_got, low, high, low_rows, high_rows, by_y, by_x
):
    mine = result.shape[1]
    core, flip = flags[0], 2 * flags[1]

    def raw(place):
        return jnp.where((place == 1) | (place == 2), jnp.where(core == 1, 3 - place, place), place)

    for h, (values, source) in enumerate(((result, parts), (result_got, parts_got))):
        first = (core if h == 0 else 1 - core) * mine
        lanes = lax.broadcasted_iota(jnp.int32, (mine, mine), 1) + first
        match = common[h * mine : (h + 1) * mine, :] == lanes
        scale = jnp.sum(jnp.where(match, values[0:1, :], 0.0), axis=1, keepdims=True)
        shift = jnp.sum(jnp.where(match, values[1:2, :], 0.0), axis=1, keepdims=True)
        grad = (scale * (source[0].astype(F32) + shift * source[1].astype(F32))).astype(BF16)
        for block in range(2 * X):
            y, x = raw((2 * h + block // X) ^ flip), raw(block % X + 0 * core)
            piece = grad[block * line : (block + 1) * line]
            by_y[rows_at(y * X + x, line), :] = piece
            by_x[rows_at(x * Y + y, line), :] = piece
    low[...] = gradient(core, by_y[mine:, :], head_keep, head_got, 0).astype(BF16)
    high[...] = gradient(core, by_x[mine:, :], head_keep, head_got, 1).astype(BF16)
    low_rows[...] = by_y[:mine, :]
    high_rows[...] = by_x[:mine, :]


def gradient(core, rows, head_keep, head_got, which):
    half, columns = head_keep.shape
    part = half // 2
    got = head_got[pl.ds(pl.multiple_of(core * half + which * part, part), part), :]
    return lax.dot_general(
        rows[:, :columns], head_keep[which * part : (which + 1) * part, :], CONTRACT_LAST, preferred_element_type=F32
    ) + lax.dot_general(rows[:, columns:], got, CONTRACT_LAST, preferred_element_type=F32)


def kept_kernel(flags, low_rows, high_rows, head_keep, head_got, low, high):
    low[...] = gradient(flags[0], low_rows[...], head_keep, head_got, 0)
    high[...] = gradient(flags[0], high_rows[...], head_keep, head_got, 1)


def on_device(policy_hidden, reference_hidden, head_weight, pair_map, response_mask):
    x0, c0, z0, y0 = (lax.axis_index(name) for name in ("x", "core", "z", "y"))
    second = c0 == 1
    swapped = (c0 ^ (y0 >> 1)) == 1
    own_rows, width = policy_hidden.shape
    half = width // 2
    part = half // 2
    columns = head_weight.shape[1]
    chip_rows = CORES * own_rows
    line = Z * chip_rows
    ring = X * line
    tokens = Y * ring
    mine = tokens // 2

    own = jnp.concatenate([policy_hidden, reference_hidden], 0)
    keep = lax.dynamic_slice_in_dim(own, c0 * half, half, 1)
    got = exchange(lax.dynamic_slice_in_dim(own, (1 - c0) * half, half, 1), across_cores)
    first_rows = jnp.where(second, got, keep)
    second_rows = jnp.where(second, keep, got)
    rows = jnp.concatenate(
        [first_rows[:own_rows], second_rows[:own_rows], first_rows[own_rows:], second_rows[own_rows:]], 0
    )
    rows, head_weight = lax.optimization_barrier((rows, head_weight))
    head_got = exchange(head_weight, across_cores)
    flags = jnp.stack([c0, c0 ^ (y0 >> 1)]).astype(jnp.int32)
    (head_keep,) = run(
        take_head,
        "take_head",
        flags,
        (head_weight,),
        [jax.ShapeDtypeStruct((half, columns), BF16)],
        in_specs=[pl.BlockSpec((half, columns), lambda i, f: (f[0], 0))],
    )

    rows = gather_z(rows)

    slot = jnp.arange(tokens, dtype=jnp.int32)

    def raw(j):
        return jnp.where(second, jnp.where(j == 0, 0, jnp.where(j == 3, 1, j + 1)), gray(j))

    sr, sc = slot % own_rows, (slot // own_rows) % CORES
    sz = z_slot((slot // chip_rows) % Z) ^ z0
    sx = gray((slot // line) % X) ^ x0
    sy = gray((slot // ring) ^ jnp.where(swapped, 2, 0)) ^ y0
    partner = jnp.take(pair_map, flat(sx, sc, sz, sy) * own_rows + sr, axis=0)
    rows, partner, head_keep = lax.optimization_barrier((rows, partner, head_keep))
    head = (head_keep, head_got)
    pr, pdev = partner % own_rows, partner // own_rows
    py, pz, pc, px = pdev % Y, (pdev // Y) % Z, (pdev // (Y * Z)) % CORES, pdev // (Y * Z * CORES)
    tail = (z_slot(pz ^ z0) * CORES + pc) * own_rows + pr
    low_place = ((raw(py ^ y0) * X + gray(px ^ x0)) * line + tail)[:, None]
    high_place = ((raw(px ^ x0) * Y + gray(py ^ y0)) * line + tail)[:, None]
    common = (((sy * X + sx) * Z + sz) * chip_rows + sc * own_rows + sr)[:, None]

    rows = rows.reshape(Z, 2, chip_rows, half).swapaxes(0, 1).reshape(2 * line, half)
    low, high = rows[:, :part], rows[:, part:]
    low_near, high_near = ring_near(low, along_x), ring_near(high, along_y)
    low_far, high_far = ring_far(low, low_near, along_x), ring_far(high, high_near, along_y)
    block = jax.ShapeDtypeStruct((ring, part), BF16)
    ra, rb, pa, pb = run(
        functools.partial(order_kernel, line),
        "order",
        flags,
        (low, low_near, low_far, high, high_near, high_far),
        [block] * 4,
    )

    ra_near, rb_near = ring_near(ra, along_y), ring_near(rb, along_x)
    pa_near, pb_near = ring_near(pa, along_y), ring_near(pb, along_x)
    ra_far, rb_far = ring_far(ra, ra_near, along_y), ring_far(rb, rb_near, along_x)
    pa_far, pb_far = ring_far(pa, pa_near, along_y), ring_far(pb, pb_near, along_x)

    logits = [jax.ShapeDtypeStruct((mine, 2 * columns), F32)] * 2
    flops = 4 * tokens * half * columns
    base = (ra, ra_near, ra_far, rb, rb_near, rb_far)
    base_keep, base_send = run(
        base_kernel,
        "base_logits",
        flags,
        (low_place, high_place, *base, *head),
        logits,
        grid=(2,),
        flops=2 * flops,
    )
    base_got = exchange(base_send, across_cores)
    policy = (pa, pa_near, pa_far, pb, pb_near, pb_far)
    policy_keep, policy_send = run(
        functools.partial(policy_kernel, line),
        "policy_logits",
        flags,
        (*policy, *head),
        logits,
        grid=(2,),
        scratch=[pltpu.VMEM((tokens, half), BF16)],
        flops=flops,
    )
    policy_got = exchange(policy_send, across_cores)

    steps = 4
    message_shape = jax.ShapeDtypeStruct((8, mine), F32)
    parts_shape = jax.ShapeDtypeStruct((2, mine, 2 * columns), BF16)
    message, parts, parts_sent = run(
        functools.partial(local_kernel, steps),
        "local_sums",
        flags,
        (common[:mine], policy_keep, policy_got, base_keep, base_got),
        [message_shape, parts_shape, parts_shape],
        grid=(steps,),
    )
    parts_got = exchange(parts_sent, across_cores)

    gathered = message
    for step in Z_STEPS:
        gathered = jnp.concatenate([gathered, exchange(gathered, along_z(step))], 0)
    (line_message,) = run(merge_kernel, "merge", flags, (gathered.reshape(Z, 8, mine),), [message_shape])
    everyone = lax.all_to_all(jnp.broadcast_to(line_message[None], (X * Y, 8, mine)), ("x", "y"), 0, 0)
    (result,) = run(result_kernel, "result", flags, (everyone, message), [message_shape])
    result_got = exchange(result, across_cores)

    rows_shape = jax.ShapeDtypeStruct((mine, 2 * columns), BF16)
    sent_shape = jax.ShapeDtypeStruct((mine, part), BF16)
    kept_shape = jax.ShapeDtypeStruct((mine, part), F32)
    operands = (common, result, result_got, parts, parts_got)
    low_sent, high_sent, low_rows, high_rows = run(
        functools.partial(sent_kernel, line),
        "gradient_sent",
        flags,
        (*operands, *head),
        [sent_shape, sent_shape, rows_shape, rows_shape],
        scratch=[pltpu.VMEM((tokens, 2 * columns), BF16)] * 2,
        flops=flops // 2,
    )
    low_got, high_got = exchange(low_sent, along_y(3, 1)), exchange(high_sent, along_x(3, 1))
    low_kept, high_kept = run(
        kept_kernel,
        "gradient_kept",
        flags,
        (low_rows, high_rows, *head),
        [kept_shape, kept_shape],
        flops=flops // 2,
    )
    low_total = low_kept + low_got.astype(F32)
    high_total = high_kept + high_got.astype(F32)
    low_total = scatter_step(low_total, along_y(1, 3))
    high_total = scatter_step(high_total, along_x(1, 3))
    low_total = scatter_step(scatter_step(low_total, along_x(3, 1)), along_x(1, 3))
    high_total = scatter_step(scatter_step(high_total, along_y(3, 1)), along_y(1, 3))
    total = jnp.concatenate([low_total, high_total], 1)
    for step in Z_STEPS[::-1]:
        total = scatter_step(total, along_z(step))

    keep = lax.dynamic_slice_in_dim(total, c0 * own_rows, own_rows, 0)
    got = exchange(lax.dynamic_slice_in_dim(total, (1 - c0) * own_rows, own_rows, 0), across_cores)
    grad = jnp.concatenate([jnp.where(second, got, keep), jnp.where(second, keep, got)], 1)
    position = ((y0 * X + x0) * Z + z0) * chip_rows + c0 * own_rows
    divergence = jnp.where(second, jnp.stack([result_got[2], result[2]]), jnp.stack([result[2], result_got[2]]))
    own_divergence = lax.dynamic_slice_in_dim(divergence.reshape(-1), position, own_rows, 0)
    weight = response_mask.astype(F32)
    return (weight * own_divergence, (weight[:, None] * grad).astype(BF16))


def solution(mesh):
    chips = Mesh(mesh.devices.reshape(X, CORES, Z, Y), AXES)
    return jax.shard_map(
        on_device,
        mesh=chips,
        in_specs=(P(AXES, None), P(AXES, None), P(None, AXES), P(), P(AXES)),
        out_specs=(P(AXES), P(AXES, None)),
        check_vma=False,
    )
```

```python
import functools

import jax
import jax.numpy as jnp
from jax import lax
from jax.experimental import pallas as pl
from jax.experimental.pallas import tpu as pltpu
from jax.sharding import Mesh, PartitionSpec as P

X, CORES, Z, Y = 4, 2, 8, 4
AXES = ("x", "core", "z", "y")
F32, BF16 = jnp.float32, jnp.bfloat16


def flat(x, c, z, y):
    return ((x * CORES + c) * Z + z) * Y + y


def exchange(value, partner):
    pairs = [
        (flat(x, c, z, y), flat(*partner(x, c, z, y)))
        for x in range(X)
        for c in range(CORES)
        for z in range(Z)
        for y in range(Y)
    ]
    return lax.ppermute(value, AXES, pairs)


def along_x(first, second):
    return lambda x, c, z, y: (x ^ (second if c else first), c, z, y)


def along_y(first, second):
    return lambda x, c, z, y: (x, c, z, y ^ (second if c else first))


def along_z(step):
    return lambda x, c, z, y: (x, c, z ^ step, y)


def across_cores(x, c, z, y):
    return (x, 1 - c, z, y)


Z_STEPS = (1, 2, 6)


def gray(j):
    return j ^ (j >> 1)


def z_slot(j):
    return j ^ ((j >> 2) << 1)


def gather_z(rows, steps):
    for step in steps:
        rows = jnp.concatenate([rows, exchange(rows, along_z(step))], 0)
    return rows


def ring_near(rows, along):
    return exchange(rows, along(1, 3))


def ring_far(rows, near, along):
    return exchange(jnp.concatenate([rows, near], 0), along(3, 1))


def scatter_step(total, partner):
    half = total.shape[0] // 2
    return total[:half] + exchange(total[half:].astype(BF16), partner).astype(F32)


CONTRACT_LAST = (((1,), (1,)), ((), ()))
VMEM_LIMIT = 20 * 1024 * 1024


WHOLE = pl.BlockSpec(memory_space=pltpu.VMEM)


def run(kernel, name, flags, operands, outputs, grid=(1,), scratch=(), in_specs=None, flops=0):
    bytes_accessed = sum(v.size * v.dtype.itemsize for v in (*operands, *outputs))
    return pl.pallas_call(
        kernel,
        out_shape=outputs,
        grid_spec=pltpu.PrefetchScalarGridSpec(
            num_scalar_prefetch=1,
            grid=grid,
            in_specs=in_specs or [WHOLE] * len(operands),
            out_specs=[WHOLE] * len(outputs),
            scratch_shapes=list(scratch),
        ),
        compiler_params=pltpu.CompilerParams(vmem_limit_bytes=VMEM_LIMIT),
        cost_estimate=pl.CostEstimate(flops=flops, bytes_accessed=bytes_accessed, transcendentals=0),
        name=name,
    )(flags, *operands)


def ring_places(core):
    return (0, 1 + core, 2 - core, 3)


def rows_at(block, count):
    return pl.ds(pl.multiple_of(block * count, count), count)


def as_column(row, start, count):
    here = lax.broadcasted_iota(jnp.int32, (count, row.shape[1]), 0) + start
    lanes = lax.broadcasted_iota(jnp.int32, (count, row.shape[1]), 1)
    return jnp.sum(jnp.where(here == lanes, row, 0.0), axis=1, keepdims=True).astype(jnp.int32)


def order_kernel(flags, low, low_near, low_far, high, high_near, high_far, ra, rb, pa, pb):
    line, width = low.shape
    part = width // 2
    places = ring_places(flags[0])
    for rows, near, far, base, policy in ((low, low_near, low_far, ra, pa), (high, high_near, high_far, rb, pb)):
        for (piece, start), place in zip(((rows, 0), (near, 0), (far, 0), (far, line)), places):
            policy[rows_at(place, line), :] = piece[start : start + line, :part]
            base[rows_at(place, line), :] = piece[start : start + line, part:]


def take_head(flags, head, keep, send, keep_done, send_done):
    half = keep.shape[0]
    copies = [
        pltpu.make_async_copy(head.at[rows_at(index, half), :], half_ref, done)
        for index, half_ref, done in ((flags[0], keep, keep_done), (1 - flags[0], send, send_done))
    ]
    for copy in copies:
        copy.start()
    for copy in copies:
        copy.wait()


def two_products(x, part, head_keep, head_got):
    def product(head):
        return jnp.dot(x[0], head[:part, :], preferred_element_type=F32) + jnp.dot(
            x[1], head[part:, :], preferred_element_type=F32
        )

    return product(head_keep), product(head_got)


def store_halves(own, other, keep, send):
    columns = own.shape[1]
    step = pl.program_id(0)

    @pl.when(step == 0)
    def _():
        keep[:, :columns] = own
        keep[:, columns:] = other

    @pl.when(step == 1)
    def _():
        send[:, :columns] = other
        send[:, columns:] = own


def base_kernel(
    flags, low_place, high_place, a, a_near, a_far, b, b_near, b_far, head_keep, head_got, keep, send
):
    count = keep.shape[0]
    first = pl.program_id(0) * count

    def pick(place, rows, near, far):
        ring = rows.shape[0]
        lanes = lax.broadcasted_iota(jnp.int32, (count, 4 * ring), 1)
        one_hot = jnp.where(as_column(place[...], first, count) == lanes, 1.0, 0.0).astype(BF16)
        total = jnp.dot(one_hot[:, :ring], rows[...], preferred_element_type=F32)
        total += jnp.dot(one_hot[:, ring : 2 * ring], near[...], preferred_element_type=F32)
        total += jnp.dot(one_hot[:, 2 * ring :], far[...], preferred_element_type=F32)
        return total.astype(BF16)

    x = (pick(low_place, a, a_near, a_far), pick(high_place, b, b_near, b_far))
    own, other = two_products(x, a.shape[1], head_keep, head_got)
    store_halves(own, other, keep, send)


def policy_kernel(line, flags, a, a_near, a_far, b, b_near, b_far, head_keep, head_got, keep, send, rows):
    step = pl.program_id(0)
    ring, part = a.shape
    mine = keep.shape[0]

    @pl.when(step == 0)
    def _():
        places = ring_places(flags[0])
        flip = 2 * flags[1]
        low = (a[...], a_near[...], a_far[:ring, :], a_far[ring:, :])
        for piece, place in zip(low, places):
            rows[rows_at(place ^ flip, ring), :part] = piece
        high = ((b, 0), (b_near, 0), (b_far, 0), (b_far, ring))
        for (piece, start), place in zip(high, places):
            for y in range(Y):
                rows[rows_at((y ^ flip) * X + place, line), part:] = piece[start + y * line : start + (y + 1) * line, :]

    x = rows[rows_at(step, mine), :]
    own, other = two_products((x[:, :part], x[:, part:]), part, head_keep, head_got)
    store_halves(own, other, keep, send)


def local_kernel(steps, flags, common, policy_keep, policy_got, base_keep, base_got, message, parts, parts_sent):
    step = pl.program_id(0)
    here = rows_at(step, policy_keep.shape[0] // steps)
    policy = policy_keep[here, :] + policy_got[here, :]
    base = base_keep[here, :] + base_got[here, :]
    difference = policy - base
    columns = policy.shape[1] // 2
    policy_peak = jnp.max(policy, axis=1, keepdims=True)
    base_peak = jnp.max(base, axis=1, keepdims=True)
    policy_exp = jnp.exp(policy - policy_peak)
    policy_total = jnp.sum(policy_exp, axis=1, keepdims=True)
    base_total = jnp.sum(jnp.exp(base - base_peak), axis=1, keepdims=True)
    center = jnp.sum(policy_exp * difference, axis=1, keepdims=True) / policy_total
    first = (policy_exp * (difference - center)).astype(BF16)
    second = policy_exp.astype(BF16)
    for i, v in enumerate((first, second)):
        parts[i, here, :] = v
        parts_sent[i, here, :columns] = v[:, columns:]
        parts_sent[i, here, columns:] = v[:, :columns]
    mine = message.shape[1]
    lanes = lax.broadcasted_iota(jnp.int32, (policy.shape[0], mine), 1) + flags[0] * mine
    match = as_column(common[...], step * (mine // steps), mine // steps) == lanes
    values = (
        policy_peak + jnp.log(policy_total),
        base_peak + jnp.log(base_total),
        center,
        policy_peak,
    )
    lines = [jnp.sum(jnp.where(match, v, 0.0), axis=0, keepdims=True) for v in values]
    block = jnp.concatenate(lines + [jnp.zeros((4, mine), F32)], axis=0)

    @pl.when(step == 0)
    def _():
        message[...] = block

    @pl.when(step > 0)
    def _():
        message[...] += block


def merged(messages):
    policy, base, mean = messages[:, 0], messages[:, 1], messages[:, 2]
    policy_peak = jnp.max(policy, axis=0, keepdims=True)
    base_peak = jnp.max(base, axis=0, keepdims=True)
    weights = jnp.exp(policy - policy_peak)
    total = jnp.sum(weights, axis=0, keepdims=True)
    base_total = jnp.sum(jnp.exp(base - base_peak), axis=0, keepdims=True)
    return (
        policy_peak + jnp.log(total),
        base_peak + jnp.log(base_total),
        jnp.sum(weights * mean, axis=0, keepdims=True) / total,
    )


def merge_kernel(flags, messages, out):
    lines = merged(messages[...])
    out[...] = jnp.concatenate([*lines, jnp.zeros((5, out.shape[1]), F32)], axis=0)


def result_kernel(flags, messages, local, out):
    policy, base, mean = merged(messages[...])
    scale = jnp.exp(local[3:4, :] - policy)
    out[...] = jnp.concatenate(
        [scale, local[2:3, :] - mean, mean - policy + base, jnp.zeros((5, out.shape[1]), F32)], axis=0
    )


def sent_kernel(
    line, flags, common, result, result_got, parts, parts_got, head_keep, head_got, low, high, low_rows, high_rows, by_y, by_x
):
    mine = result.shape[1]
    core, flip = flags[0], 2 * flags[1]

    def raw(place):
        return jnp.where((place == 1) | (place == 2), jnp.where(core == 1, 3 - place, place), place)

    for h, (values, source) in enumerate(((result, parts), (result_got, parts_got))):
        first = (core if h == 0 else 1 - core) * mine
        lanes = lax.broadcasted_iota(jnp.int32, (mine, mine), 1) + first
        match = as_column(common[:, h * mine : (h + 1) * mine], 0, mine) == lanes
        scale = jnp.sum(jnp.where(match, values[0:1, :], 0.0), axis=1, keepdims=True)
        shift = jnp.sum(jnp.where(match, values[1:2, :], 0.0), axis=1, keepdims=True)
        grad = (scale * (source[0].astype(F32) + shift * source[1].astype(F32))).astype(BF16)
        for block in range(2 * X):
            y, x = raw((2 * h + block // X) ^ flip), raw(block % X + 0 * core)
            piece = grad[block * line : (block + 1) * line]
            by_y[rows_at(y * X + x, line), :] = piece
            by_x[rows_at(x * Y + y, line), :] = piece
    low[...] = gradient(by_y[mine:, :], head_keep, head_got, 0).astype(BF16)
    high[...] = gradient(by_x[mine:, :], head_keep, head_got, 1).astype(BF16)
    low_rows[...] = by_y[:mine, :]
    high_rows[...] = by_x[:mine, :]


def gradient(rows, head_keep, head_got, which):
    columns = head_keep.shape[1]
    part = head_keep.shape[0] // 2
    span = slice(which * part, (which + 1) * part)
    return lax.dot_general(
        rows[:, :columns], head_keep[span, :], CONTRACT_LAST, preferred_element_type=F32
    ) + lax.dot_general(rows[:, columns:], head_got[span, :], CONTRACT_LAST, preferred_element_type=F32)


def kept_kernel(flags, low_rows, high_rows, head_keep, head_got, low, high):
    low[...] = gradient(low_rows[...], head_keep, head_got, 0)
    high[...] = gradient(high_rows[...], head_keep, head_got, 1)


def on_device(policy_hidden, reference_hidden, head_weight, pair_map, response_mask):
    x0, c0, z0, y0 = (lax.axis_index(name) for name in ("x", "core", "z", "y"))
    second = c0 == 1
    swapped = (c0 ^ (y0 >> 1)) == 1
    own_rows, width = policy_hidden.shape
    half = width // 2
    part = half // 2
    columns = head_weight.shape[1]
    chip_rows = CORES * own_rows
    line = Z * chip_rows
    ring = X * line
    tokens = Y * ring
    mine = tokens // 2

    def side_by_side(first):
        p = lax.dynamic_slice_in_dim(policy_hidden, first, half, 1)
        r = lax.dynamic_slice_in_dim(reference_hidden, first, half, 1)
        return jnp.concatenate([p[:, :part], r[:, :part], p[:, part:], r[:, part:]], 1)

    keep = side_by_side(c0 * half)
    got = exchange(side_by_side((1 - c0) * half), across_cores)
    rows = jnp.concatenate([jnp.where(second, got, keep), jnp.where(second, keep, got)], 0)
    rows, head_weight = lax.optimization_barrier((rows, head_weight))
    flags = jnp.stack([c0, c0 ^ (y0 >> 1)]).astype(jnp.int32)
    head_shape = jax.ShapeDtypeStruct((half, columns), BF16)
    head_keep, head_send = run(
        take_head,
        "take_head",
        flags,
        (head_weight,),
        [head_shape, head_shape],
        in_specs=[pl.BlockSpec(memory_space=pltpu.HBM)],
        scratch=[pltpu.SemaphoreType.DMA] * 2,
    )
    slot = jnp.arange(tokens, dtype=jnp.int32)[None]

    def raw(j):
        return jnp.where(second, jnp.where(j == 0, 0, jnp.where(j == 3, 1, j + 1)), gray(j))

    sr, sc = slot % own_rows, (slot // own_rows) % CORES
    sz = z_slot((slot // chip_rows) % Z) ^ z0
    sx = gray((slot // line) % X) ^ x0
    sy = gray((slot // ring) ^ jnp.where(swapped, 2, 0)) ^ y0
    partner = jnp.take(pair_map, flat(sx, sc, sz, sy) * own_rows + sr, axis=0)
    rows = gather_z(rows, Z_STEPS[:1])
    rows, partner = lax.optimization_barrier((rows, partner))
    rows = gather_z(rows, Z_STEPS[1:2])
    rows, head_keep, head_send = lax.optimization_barrier((rows, head_keep, head_send))
    head = (head_keep, exchange(head_send, across_cores))
    rows = gather_z(rows, Z_STEPS[2:])
    pr, pdev = partner % own_rows, partner // own_rows
    py, pz, pc, px = pdev % Y, (pdev // Y) % Z, (pdev // (Y * Z)) % CORES, pdev // (Y * Z * CORES)
    tail = (z_slot(pz ^ z0) * CORES + pc) * own_rows + pr
    low_place = ((raw(py ^ y0) * X + gray(px ^ x0)) * line + tail).astype(F32)
    high_place = ((raw(px ^ x0) * Y + gray(py ^ y0)) * line + tail).astype(F32)
    common = (((sy * X + sx) * Z + sz) * chip_rows + sc * own_rows + sr).astype(F32)

    low, high = rows[:, :half], rows[:, half:]
    low_near, high_near = ring_near(low, along_x), ring_near(high, along_y)
    low_far, high_far = ring_far(low, low_near, along_x), ring_far(high, high_near, along_y)
    block = jax.ShapeDtypeStruct((ring, part), BF16)
    ra, rb, pa, pb = run(
        order_kernel,
        "order",
        flags,
        (low, low_near, low_far, high, high_near, high_far),
        [block] * 4,
    )

    ra_near, rb_near = ring_near(ra, along_y), ring_near(rb, along_x)
    pa_near, pb_near = ring_near(pa, along_y), ring_near(pb, along_x)
    ra_far, rb_far = ring_far(ra, ra_near, along_y), ring_far(rb, rb_near, along_x)
    pa_far, pb_far = ring_far(pa, pa_near, along_y), ring_far(pb, pb_near, along_x)

    logits = [jax.ShapeDtypeStruct((mine, 2 * columns), F32)] * 2
    flops = 4 * tokens * half * columns
    base = (ra, ra_near, ra_far, rb, rb_near, rb_far)
    base_keep, base_send = run(
        base_kernel,
        "base_logits",
        flags,
        (low_place, high_place, *base, *head),
        logits,
        grid=(2,),
        flops=2 * flops,
    )
    base_got = exchange(base_send, across_cores)
    policy = (pa, pa_near, pa_far, pb, pb_near, pb_far)
    policy_keep, policy_send = run(
        functools.partial(policy_kernel, line),
        "policy_logits",
        flags,
        (*policy, *head),
        logits,
        grid=(2,),
        scratch=[pltpu.VMEM((tokens, half), BF16)],
        flops=flops,
    )
    policy_got = exchange(policy_send, across_cores)

    steps = 4
    message_shape = jax.ShapeDtypeStruct((8, mine), F32)
    parts_shape = jax.ShapeDtypeStruct((2, mine, 2 * columns), BF16)
    message, parts, parts_sent = run(
        functools.partial(local_kernel, steps),
        "local_sums",
        flags,
        (common[:, :mine], policy_keep, policy_got, base_keep, base_got),
        [message_shape, parts_shape, parts_shape],
        grid=(steps,),
    )
    parts_got = exchange(parts_sent, across_cores)

    gathered = message
    for step in Z_STEPS:
        gathered = jnp.concatenate([gathered, exchange(gathered, along_z(step))], 0)
    (line_message,) = run(merge_kernel, "merge", flags, (gathered.reshape(Z, 8, mine),), [message_shape])
    everyone = lax.all_to_all(jnp.broadcast_to(line_message[None], (X * Y, 8, mine)), ("x", "y"), 0, 0)
    (result,) = run(result_kernel, "result", flags, (everyone, message), [message_shape])
    result_got = exchange(result, across_cores)

    rows_shape = jax.ShapeDtypeStruct((mine, 2 * columns), BF16)
    sent_shape = jax.ShapeDtypeStruct((mine, part), BF16)
    kept_shape = jax.ShapeDtypeStruct((mine, part), F32)
    operands = (common, result, result_got, parts, parts_got)
    low_sent, high_sent, low_rows, high_rows = run(
        functools.partial(sent_kernel, line),
        "gradient_sent",
        flags,
        (*operands, *head),
        [sent_shape, sent_shape, rows_shape, rows_shape],
        scratch=[pltpu.VMEM((tokens, 2 * columns), BF16)] * 2,
        flops=flops // 2,
    )
    low_got, high_got = exchange(low_sent, along_y(3, 1)), exchange(high_sent, along_x(3, 1))
    low_kept, high_kept = run(
        kept_kernel,
        "gradient_kept",
        flags,
        (low_rows, high_rows, *head),
        [kept_shape, kept_shape],
        flops=flops // 2,
    )
    low_total = low_kept + low_got.astype(F32)
    high_total = high_kept + high_got.astype(F32)
    low_total = scatter_step(low_total, along_y(1, 3))
    high_total = scatter_step(high_total, along_x(1, 3))
    low_total = scatter_step(scatter_step(low_total, along_x(3, 1)), along_x(1, 3))
    high_total = scatter_step(scatter_step(high_total, along_y(3, 1)), along_y(1, 3))
    total = jnp.concatenate([low_total, high_total], 1)
    for step in Z_STEPS[::-1]:
        total = scatter_step(total, along_z(step))

    keep = lax.dynamic_slice_in_dim(total, c0 * own_rows, own_rows, 0)
    got = exchange(lax.dynamic_slice_in_dim(total, (1 - c0) * own_rows, own_rows, 0), across_cores)
    grad = jnp.concatenate([jnp.where(second, got, keep), jnp.where(second, keep, got)], 1)
    position = ((y0 * X + x0) * Z + z0) * chip_rows + c0 * own_rows
    divergence = jnp.where(second, jnp.stack([result_got[2], result[2]]), jnp.stack([result[2], result_got[2]]))
    own_divergence = lax.dynamic_slice_in_dim(divergence.reshape(-1), position, own_rows, 0)
    weight = response_mask.astype(F32)
    return (weight * own_divergence, (weight[:, None] * grad).astype(BF16))


def solution(mesh):
    chips = Mesh(mesh.devices.reshape(X, CORES, Z, Y), AXES)
    return jax.shard_map(
        on_device,
        mesh=chips,
        in_specs=(P(AXES, None), P(AXES, None), P(None, AXES), P(), P(AXES)),
        out_specs=(P(AXES), P(AXES, None)),
        check_vma=False,
    )
```

```python
import functools

import jax
import jax.numpy as jnp
from jax import lax
from jax.experimental import pallas as pl
from jax.experimental.pallas import tpu as pltpu
from jax.sharding import Mesh, PartitionSpec as P

X, CORES, Z, Y = 4, 2, 8, 4
AXES = ("x", "core", "z", "y")
F32, BF16 = jnp.float32, jnp.bfloat16


def flat(x, c, z, y):
    return ((x * CORES + c) * Z + z) * Y + y


def exchange(value, partner):
    pairs = [
        (flat(x, c, z, y), flat(*partner(x, c, z, y)))
        for x in range(X)
        for c in range(CORES)
        for z in range(Z)
        for y in range(Y)
    ]
    return lax.ppermute(value, AXES, pairs)


def along_x(first, second):
    return lambda x, c, z, y: (x ^ (second if c else first), c, z, y)


def along_y(first, second):
    return lambda x, c, z, y: (x, c, z, y ^ (second if c else first))


def along_z(step):
    return lambda x, c, z, y: (x, c, z ^ step, y)


def across_cores(x, c, z, y):
    return (x, 1 - c, z, y)


Z_STEPS = (2, 6, 1)


def gray(j):
    return j ^ (j >> 1)


def z_slot(j):
    return (((j >> 1) ^ (j >> 2)) & 1) | ((j >> 1) & 2) | ((j & 1) << 2)


def z_offset(slot):
    return (slot >> 2) ^ ((slot & 1) * 2) ^ (((slot >> 1) & 1) * 6)


def gather_z(rows, steps):
    for step in steps:
        rows = jnp.concatenate([rows, exchange(rows, along_z(step))], 0)
    return rows


def ring_near(rows, along):
    return exchange(rows, along(1, 3))


def ring_far(rows, near, along):
    return exchange(jnp.concatenate([rows, near], 0), along(3, 1))


def scatter_step(total, partner):
    half = total.shape[0] // 2
    return total[:half] + exchange(total[half:].astype(BF16), partner).astype(F32)


CONTRACT_LAST = (((1,), (1,)), ((), ()))
VMEM_LIMIT = 20 * 1024 * 1024


WHOLE = pl.BlockSpec(memory_space=pltpu.VMEM)


def run(kernel, name, flags, operands, outputs, grid=(1,), scratch=(), in_specs=None, flops=0):
    bytes_accessed = sum(v.size * v.dtype.itemsize for v in (*operands, *outputs))
    return pl.pallas_call(
        kernel,
        out_shape=outputs,
        grid_spec=pltpu.PrefetchScalarGridSpec(
            num_scalar_prefetch=1,
            grid=grid,
            in_specs=in_specs or [WHOLE] * len(operands),
            out_specs=[WHOLE] * len(outputs),
            scratch_shapes=list(scratch),
        ),
        compiler_params=pltpu.CompilerParams(vmem_limit_bytes=VMEM_LIMIT),
        cost_estimate=pl.CostEstimate(flops=flops, bytes_accessed=bytes_accessed, transcendentals=0),
        name=name,
    )(flags, *operands)


def ring_places(core):
    return (0, 1 + core, 2 - core, 3)


def rows_at(block, count):
    return pl.ds(pl.multiple_of(block * count, count), count)


def as_column(row, start, count):
    here = lax.broadcasted_iota(jnp.int32, (count, row.shape[1]), 0) + start
    lanes = lax.broadcasted_iota(jnp.int32, (count, row.shape[1]), 1)
    return jnp.sum(jnp.where(here == lanes, row, 0.0), axis=1, keepdims=True).astype(jnp.int32)


def order_kernel(flags, low, low_near, low_far, high, high_near, high_far, a, b):
    line = low.shape[0]
    places = ring_places(flags[0])
    for rows, near, far, out in ((low, low_near, low_far, a), (high, high_near, high_far, b)):
        for (piece, start), place in zip(((rows, 0), (near, 0), (far, 0), (far, line)), places):
            out[rows_at(place, line), :] = piece[start : start + line, :]


def take_head(flags, head, keep, send, keep_done, send_done):
    half = keep.shape[0]
    copies = [
        pltpu.make_async_copy(head.at[rows_at(index, half), :], half_ref, done)
        for index, half_ref, done in ((flags[0], keep, keep_done), (1 - flags[0], send, send_done))
    ]
    for copy in copies:
        copy.start()
    for copy in copies:
        copy.wait()


def two_products(x, part, head_keep, head_got):
    def product(head):
        return jnp.dot(x[0], head[:part, :], preferred_element_type=F32) + jnp.dot(
            x[1], head[part:, :], preferred_element_type=F32
        )

    return product(head_keep), product(head_got)


def store_halves(own, other, keep, send):
    columns = own.shape[1]
    step = pl.program_id(0)

    @pl.when(step == 0)
    def _():
        keep[:, :columns] = own
        keep[:, columns:] = other

    @pl.when(step == 1)
    def _():
        send[:, :columns] = other
        send[:, columns:] = own


def base_kernel(
    flags, low_place, high_place, a, a_near, a_far, b, b_near, b_far, head_keep, head_got, keep, send
):
    count = keep.shape[0]
    first = pl.program_id(0) * count

    def pick(place, rows, near, far):
        ring, part = far.shape[0] // 2, far.shape[1]
        lanes = lax.broadcasted_iota(jnp.int32, (count, 4 * ring), 1)
        one_hot = jnp.where(as_column(place[...], first, count) == lanes, 1.0, 0.0).astype(BF16)
        total = jnp.dot(one_hot[:, :ring], rows[...], preferred_element_type=F32)
        total += jnp.dot(one_hot[:, ring : 2 * ring], near[...], preferred_element_type=F32)
        total += jnp.dot(one_hot[:, 2 * ring :], far[...], preferred_element_type=F32)
        return total.astype(BF16)

    x = (pick(low_place, a, a_near, a_far), pick(high_place, b, b_near, b_far))
    own, other = two_products(x, a_far.shape[1], head_keep, head_got)
    store_halves(own, other, keep, send)


def policy_kernel(line, flags, a, a_near, a_far, b, b_near, b_far, head_keep, head_got, keep, send, rows):
    step = pl.program_id(0)
    ring, part = a.shape[0], a_far.shape[1]
    mine = keep.shape[0]

    @pl.when(step == 0)
    def _():
        places = ring_places(flags[0])
        flip = 2 * flags[1]
        low = (a[...], a_near[...], a_far[:ring, :], a_far[ring:, :])
        for piece, place in zip(low, places):
            rows[rows_at(place ^ flip, ring), :part] = piece
        high = ((b, 0), (b_near, 0), (b_far, 0), (b_far, ring))
        for (piece, start), place in zip(high, places):
            for y in range(Y):
                rows[rows_at((y ^ flip) * X + place, line), part:] = piece[
                    start + y * line : start + (y + 1) * line, :part
                ]

    x = rows[rows_at(step, mine), :]
    own, other = two_products((x[:, :part], x[:, part:]), part, head_keep, head_got)
    store_halves(own, other, keep, send)


def local_kernel(steps, flags, common, policy_keep, policy_got, base_keep, base_got, message, parts, parts_sent):
    step = pl.program_id(0)
    here = rows_at(step, policy_keep.shape[0] // steps)
    policy = policy_keep[here, :] + policy_got[here, :]
    base = base_keep[here, :] + base_got[here, :]
    difference = policy - base
    columns = policy.shape[1] // 2
    policy_peak = jnp.max(policy, axis=1, keepdims=True)
    base_peak = jnp.max(base, axis=1, keepdims=True)
    policy_exp = jnp.exp(policy - policy_peak)
    policy_total = jnp.sum(policy_exp, axis=1, keepdims=True)
    base_total = jnp.sum(jnp.exp(base - base_peak), axis=1, keepdims=True)
    center = jnp.sum(policy_exp * difference, axis=1, keepdims=True) / policy_total
    first = (policy_exp * (difference - center)).astype(BF16)
    second = policy_exp.astype(BF16)
    for i, v in enumerate((first, second)):
        parts[i, here, :] = v
        parts_sent[i, here, :columns] = v[:, columns:]
        parts_sent[i, here, columns:] = v[:, :columns]
    mine = message.shape[1]
    lanes = lax.broadcasted_iota(jnp.int32, (policy.shape[0], mine), 1) + flags[0] * mine
    match = as_column(common[...], step * (mine // steps), mine // steps) == lanes
    values = (
        policy_peak + jnp.log(policy_total),
        base_peak + jnp.log(base_total),
        center,
        policy_peak,
    )
    lines = [jnp.sum(jnp.where(match, v, 0.0), axis=0, keepdims=True) for v in values]
    block = jnp.concatenate(lines + [jnp.zeros((4, mine), F32)], axis=0)

    @pl.when(step == 0)
    def _():
        message[...] = block

    @pl.when(step > 0)
    def _():
        message[...] += block


def merged(messages):
    policy, base, mean = messages[:, 0], messages[:, 1], messages[:, 2]
    policy_peak = jnp.max(policy, axis=0, keepdims=True)
    base_peak = jnp.max(base, axis=0, keepdims=True)
    weights = jnp.exp(policy - policy_peak)
    total = jnp.sum(weights, axis=0, keepdims=True)
    base_total = jnp.sum(jnp.exp(base - base_peak), axis=0, keepdims=True)
    return (
        policy_peak + jnp.log(total),
        base_peak + jnp.log(base_total),
        jnp.sum(weights * mean, axis=0, keepdims=True) / total,
    )


def merge_kernel(flags, messages, out):
    lines = merged(messages[...])
    out[...] = jnp.concatenate([*lines, jnp.zeros((5, out.shape[1]), F32)], axis=0)


def result_kernel(flags, messages, local, out):
    policy, base, mean = merged(messages[...])
    scale = jnp.exp(local[3:4, :] - policy)
    out[...] = jnp.concatenate(
        [scale, local[2:3, :] - mean, mean - policy + base, jnp.zeros((5, out.shape[1]), F32)], axis=0
    )


def sent_kernel(
    line, flags, common, result, result_got, parts, parts_got, head_keep, head_got, low, by_y, by_x
):
    mine = result.shape[1]
    core, flip = flags[0], 2 * flags[1]

    def raw(place):
        return jnp.where((place == 1) | (place == 2), jnp.where(core == 1, 3 - place, place), place)

    for h, (values, source) in enumerate(((result, parts), (result_got, parts_got))):
        first = (core if h == 0 else 1 - core) * mine
        lanes = lax.broadcasted_iota(jnp.int32, (mine, mine), 1) + first
        match = as_column(common[:, h * mine : (h + 1) * mine], 0, mine) == lanes
        scale = jnp.sum(jnp.where(match, values[0:1, :], 0.0), axis=1, keepdims=True)
        shift = jnp.sum(jnp.where(match, values[1:2, :], 0.0), axis=1, keepdims=True)
        grad = (scale * (source[0].astype(F32) + shift * source[1].astype(F32))).astype(BF16)
        for block in range(2 * X):
            y, x = raw((2 * h + block // X) ^ flip), raw(block % X + 0 * core)
            piece = grad[block * line : (block + 1) * line]
            by_y[rows_at(y * X + x, line), :] = piece
            by_x[rows_at(x * Y + y, line), :] = piece
    low[...] = gradient(by_y[mine:, :], head_keep, head_got, 0).astype(BF16)


def high_kernel(flags, by_x, head_keep, head_got, high):
    high[...] = gradient(by_x[high.shape[0] :, :], head_keep, head_got, 1).astype(BF16)


def gradient(rows, head_keep, head_got, which):
    columns = head_keep.shape[1]
    part = head_keep.shape[0] // 2
    span = slice(which * part, (which + 1) * part)
    return lax.dot_general(
        rows[:, :columns], head_keep[span, :], CONTRACT_LAST, preferred_element_type=F32
    ) + lax.dot_general(rows[:, columns:], head_got[span, :], CONTRACT_LAST, preferred_element_type=F32)


def kept_kernel(flags, by_y, by_x, head_keep, head_got, low, high):
    mine = low.shape[0]
    low[...] = gradient(by_y[:mine, :], head_keep, head_got, 0)
    high[...] = gradient(by_x[:mine, :], head_keep, head_got, 1)


def on_device(policy_hidden, reference_hidden, head_weight, pair_map, response_mask):
    x0, c0, z0, y0 = (lax.axis_index(name) for name in ("x", "core", "z", "y"))
    second = c0 == 1
    swapped = (c0 ^ (y0 >> 1)) == 1
    own_rows, width = policy_hidden.shape
    half = width // 2
    part = half // 2
    columns = head_weight.shape[1]
    chip_rows = CORES * own_rows
    line = Z * chip_rows
    ring = X * line
    tokens = Y * ring
    mine = tokens // 2

    def side_by_side(first):
        p = lax.dynamic_slice_in_dim(policy_hidden, first, half, 1)
        r = lax.dynamic_slice_in_dim(reference_hidden, first, half, 1)
        return jnp.concatenate([p[:, :part], r[:, :part], p[:, part:], r[:, part:]], 1)

    keep = side_by_side(c0 * half)
    got = exchange(side_by_side((1 - c0) * half), across_cores)
    rows = jnp.concatenate([jnp.where(second, got, keep), jnp.where(second, keep, got)], 0)
    rows, head_weight = lax.optimization_barrier((rows, head_weight))
    flags = jnp.stack([c0, c0 ^ (y0 >> 1)]).astype(jnp.int32)
    head_shape = jax.ShapeDtypeStruct((half, columns), BF16)
    slot = jnp.arange(tokens, dtype=jnp.int32)[None]

    def raw(j):
        return jnp.where(second, jnp.where(j == 0, 0, jnp.where(j == 3, 1, j + 1)), gray(j))

    sr, sc = slot % own_rows, (slot // own_rows) % CORES
    sz = z_offset((slot // chip_rows) % Z) ^ z0
    sx = gray((slot // line) % X) ^ x0
    sy = gray((slot // ring) ^ jnp.where(swapped, 2, 0)) ^ y0
    own_token = flat(sx, sc, sz, sy) * own_rows + sr
    rows = gather_z(rows, Z_STEPS[:1])
    rows, own_token = lax.optimization_barrier((rows, own_token))
    partner = jnp.take(pair_map, own_token, axis=0)
    rows = gather_z(rows, Z_STEPS[1:2])
    rows, partner, head_weight = lax.optimization_barrier((rows, partner, head_weight))
    head_keep, head_send = run(
        take_head,
        "take_head",
        flags,
        (head_weight,),
        [head_shape, head_shape],
        in_specs=[pl.BlockSpec(memory_space=pltpu.HBM)],
        scratch=[pltpu.SemaphoreType.DMA] * 2,
    )
    rows = gather_z(rows, Z_STEPS[2:])
    rows, head_keep, head_send = lax.optimization_barrier((rows, head_keep, head_send))
    head = (head_keep, exchange(head_send, across_cores))
    pr, pdev = partner % own_rows, partner // own_rows
    py, pz, pc, px = pdev % Y, (pdev // Y) % Z, (pdev // (Y * Z)) % CORES, pdev // (Y * Z * CORES)
    tail = (z_slot(pz ^ z0) * CORES + pc) * own_rows + pr
    low_place = ((raw(py ^ y0) * X + gray(px ^ x0)) * line + tail).astype(F32)
    high_place = ((raw(px ^ x0) * Y + gray(py ^ y0)) * line + tail).astype(F32)
    common = (((sy * X + sx) * Z + sz) * chip_rows + sc * own_rows + sr).astype(F32)

    spans = [(rows[:, part:half], rows[:, half + part :]), (rows[:, :part], rows[:, half : half + part])]
    gathered = []
    for low, high in spans:
        low_near, high_near = ring_near(low, along_x), ring_near(high, along_y)
        low_far, high_far = ring_far(low, low_near, along_x), ring_far(high, high_near, along_y)
        a, b = run(
            order_kernel,
            "order",
            flags,
            (low, low_near, low_far, high, high_near, high_far),
            [jax.ShapeDtypeStruct((ring, part), BF16)] * 2,
        )
        a_near, b_near = ring_near(a, along_y), ring_near(b, along_x)
        a_far, b_far = ring_far(a, a_near, along_y), ring_far(b, b_near, along_x)
        gathered.append((a, a_near, a_far, b, b_near, b_far))
    base, policy = gathered

    logits = [jax.ShapeDtypeStruct((mine, 2 * columns), F32)] * 2
    flops = 4 * tokens * half * columns
    base_keep, base_send = run(
        base_kernel,
        "base_logits",
        flags,
        (low_place, high_place, *base, *head),
        logits,
        grid=(2,),
        flops=2 * flops,
    )
    base_got = exchange(base_send, across_cores)
    policy_keep, policy_send = run(
        functools.partial(policy_kernel, line),
        "policy_logits",
        flags,
        (*policy, *head),
        logits,
        grid=(2,),
        scratch=[pltpu.VMEM((tokens, half), BF16)],
        flops=flops,
    )
    policy_got = exchange(policy_send, across_cores)

    steps = 4
    message_shape = jax.ShapeDtypeStruct((8, mine), F32)
    parts_shape = jax.ShapeDtypeStruct((2, mine, 2 * columns), BF16)
    message, parts, parts_sent = run(
        functools.partial(local_kernel, steps),
        "local_sums",
        flags,
        (common[:, :mine], policy_keep, policy_got, base_keep, base_got),
        [message_shape, parts_shape, parts_shape],
        grid=(steps,),
    )
    parts_got = exchange(parts_sent, across_cores)

    gathered = message
    for step in Z_STEPS:
        gathered = jnp.concatenate([gathered, exchange(gathered, along_z(step))], 0)
    (line_message,) = run(merge_kernel, "merge", flags, (gathered.reshape(Z, 8, mine),), [message_shape])
    everyone = lax.all_to_all(jnp.broadcast_to(line_message[None], (X * Y, 8, mine)), ("x", "y"), 0, 0)
    (result,) = run(result_kernel, "result", flags, (everyone, message), [message_shape])
    result_got = exchange(result, across_cores)

    rows_shape = jax.ShapeDtypeStruct((tokens, 2 * columns), BF16)
    sent_shape = jax.ShapeDtypeStruct((mine, part), BF16)
    kept_shape = jax.ShapeDtypeStruct((mine, part), F32)
    low_sent, by_y, by_x = run(
        functools.partial(sent_kernel, line),
        "gradient_sent_low",
        flags,
        (common, result, result_got, parts, parts_got, *head),
        [sent_shape, rows_shape, rows_shape],
        flops=flops // 4,
    )
    low_got = exchange(low_sent, along_y(3, 1))
    (high_sent,) = run(high_kernel, "gradient_sent_high", flags, (by_x, *head), [sent_shape], flops=flops // 4)
    high_got = exchange(high_sent, along_x(3, 1))
    low_kept, high_kept = run(
        kept_kernel, "gradient_kept", flags, (by_y, by_x, *head), [kept_shape, kept_shape], flops=flops // 2
    )
    low_total = low_kept + low_got.astype(F32)
    high_total = high_kept + high_got.astype(F32)
    low_total = scatter_step(low_total, along_y(1, 3))
    high_total = scatter_step(high_total, along_x(1, 3))
    low_total = scatter_step(scatter_step(low_total, along_x(3, 1)), along_x(1, 3))
    high_total = scatter_step(scatter_step(high_total, along_y(3, 1)), along_y(1, 3))
    total = jnp.concatenate([low_total, high_total], 1)
    for step in Z_STEPS[::-1]:
        total = scatter_step(total, along_z(step))

    keep = lax.dynamic_slice_in_dim(total, c0 * own_rows, own_rows, 0)
    got = exchange(lax.dynamic_slice_in_dim(total, (1 - c0) * own_rows, own_rows, 0), across_cores)
    grad = jnp.concatenate([jnp.where(second, got, keep), jnp.where(second, keep, got)], 1)
    position = ((y0 * X + x0) * Z + z0) * chip_rows + c0 * own_rows
    divergence = jnp.where(second, jnp.stack([result_got[2], result[2]]), jnp.stack([result[2], result_got[2]]))
    own_divergence = lax.dynamic_slice_in_dim(divergence.reshape(-1), position, own_rows, 0)
    weight = response_mask.astype(F32)
    return (weight * own_divergence, (weight[:, None] * grad).astype(BF16))


def solution(mesh):
    chips = Mesh(mesh.devices.reshape(X, CORES, Z, Y), AXES)
    return jax.shard_map(
        on_device,
        mesh=chips,
        in_specs=(P(AXES, None), P(AXES, None), P(None, AXES), P(), P(AXES)),
        out_specs=(P(AXES), P(AXES, None)),
        check_vma=False,
    )
```

```python
import functools

import jax
import jax.numpy as jnp
from jax import lax
from jax.experimental import pallas as pl
from jax.experimental.pallas import tpu as pltpu
from jax.sharding import Mesh, PartitionSpec as P

X, CORES, Z, Y = 4, 2, 8, 4
AXES = ("x", "core", "z", "y")
F32, BF16 = jnp.float32, jnp.bfloat16


def flat(x, c, z, y):
    return ((x * CORES + c) * Z + z) * Y + y


def exchange(value, partner):
    pairs = [
        (flat(x, c, z, y), flat(*partner(x, c, z, y)))
        for x in range(X)
        for c in range(CORES)
        for z in range(Z)
        for y in range(Y)
    ]
    return lax.ppermute(value, AXES, pairs)


def along_x(first, second):
    return lambda x, c, z, y: (x ^ (second if c else first), c, z, y)


def along_y(first, second):
    return lambda x, c, z, y: (x, c, z, y ^ (second if c else first))


def along_z(step):
    return lambda x, c, z, y: (x, c, z ^ step, y)


def across_cores(x, c, z, y):
    return (x, 1 - c, z, y)


Z_STEPS = (2, 6, 1)


def gray(j):
    return j ^ (j >> 1)


def z_slot(j):
    return (((j >> 1) ^ (j >> 2)) & 1) | ((j >> 1) & 2) | ((j & 1) << 2)


def z_offset(slot):
    return (slot >> 2) ^ ((slot & 1) * 2) ^ (((slot >> 1) & 1) * 6)


def gather_z(rows, steps):
    for step in steps:
        rows = jnp.concatenate([rows, exchange(rows, along_z(step))], 0)
    return rows


def ring_near(rows, along):
    return exchange(rows, along(1, 3))


def ring_far(rows, near, along):
    return exchange(jnp.concatenate([rows, near], 0), along(3, 1))


def scatter_step(total, partner):
    half = total.shape[0] // 2
    return total[:half] + exchange(total[half:].astype(BF16), partner).astype(F32)


CONTRACT_LAST = (((1,), (1,)), ((), ()))
VMEM_LIMIT = 20 * 1024 * 1024


WHOLE = pl.BlockSpec(memory_space=pltpu.VMEM)


def run(kernel, name, flags, operands, outputs, grid=(1,), scratch=(), in_specs=None, flops=0):
    bytes_accessed = sum(v.size * v.dtype.itemsize for v in (*operands, *outputs))
    return pl.pallas_call(
        kernel,
        out_shape=outputs,
        grid_spec=pltpu.PrefetchScalarGridSpec(
            num_scalar_prefetch=1,
            grid=grid,
            in_specs=in_specs or [WHOLE] * len(operands),
            out_specs=[WHOLE] * len(outputs),
            scratch_shapes=list(scratch),
        ),
        compiler_params=pltpu.CompilerParams(vmem_limit_bytes=VMEM_LIMIT),
        cost_estimate=pl.CostEstimate(flops=flops, bytes_accessed=bytes_accessed, transcendentals=0),
        name=name,
    )(flags, *operands)


def ring_places(core):
    return (0, 1 + core, 2 - core, 3)


def rows_at(block, count):
    return pl.ds(pl.multiple_of(block * count, count), count)


def as_column(row, start, count):
    here = lax.broadcasted_iota(jnp.int32, (count, row.shape[1]), 0) + start
    lanes = lax.broadcasted_iota(jnp.int32, (count, row.shape[1]), 1)
    return jnp.sum(jnp.where(here == lanes, row, 0.0), axis=1, keepdims=True).astype(jnp.int32)


def order_kernel(flags, low, low_near, low_far, high, high_near, high_far, a, b):
    line = low.shape[0]
    places = ring_places(flags[0])
    for rows, near, far, out in ((low, low_near, low_far, a), (high, high_near, high_far, b)):
        for (piece, start), place in zip(((rows, 0), (near, 0), (far, 0), (far, line)), places):
            out[rows_at(place, line), :] = piece[start : start + line, :]


def take_head(flags, head, keep, send, keep_done, send_done):
    half = keep.shape[0]
    copies = [
        pltpu.make_async_copy(head.at[rows_at(index, half), :], half_ref, done)
        for index, half_ref, done in ((flags[0], keep, keep_done), (1 - flags[0], send, send_done))
    ]
    for copy in copies:
        copy.start()
    for copy in copies:
        copy.wait()


def two_products(x, part, head_keep, head_got):
    def product(head):
        return jnp.dot(x[0], head[:part, :], preferred_element_type=F32) + jnp.dot(
            x[1], head[part:, :], preferred_element_type=F32
        )

    return product(head_keep), product(head_got)


def store_halves(own, other, keep, send):
    columns = own.shape[1]
    step = pl.program_id(0)

    @pl.when(step == 0)
    def _():
        keep[:, :columns] = own
        keep[:, columns:] = other

    @pl.when(step == 1)
    def _():
        send[:, :columns] = other
        send[:, columns:] = own


def base_kernel(
    flags, low_place, high_place, a, a_near, a_far, b, b_near, b_far, head_keep, head_got, keep, send
):
    count = keep.shape[0]
    first = pl.program_id(0) * count

    def pick(place, rows, near, far):
        ring, part = far.shape[0] // 2, far.shape[1]
        lanes = lax.broadcasted_iota(jnp.int32, (count, 4 * ring), 1)
        one_hot = jnp.where(as_column(place[...], first, count) == lanes, 1.0, 0.0).astype(BF16)
        total = jnp.dot(one_hot[:, :ring], rows[...], preferred_element_type=F32)
        total += jnp.dot(one_hot[:, ring : 2 * ring], near[...], preferred_element_type=F32)
        total += jnp.dot(one_hot[:, 2 * ring :], far[...], preferred_element_type=F32)
        return total.astype(BF16)

    x = (pick(low_place, a, a_near, a_far), pick(high_place, b, b_near, b_far))
    own, other = two_products(x, a_far.shape[1], head_keep, head_got)
    store_halves(own, other, keep, send)


def policy_kernel(line, flags, a, a_near, a_far, b, b_near, b_far, head_keep, head_got, keep, send, rows):
    step = pl.program_id(0)
    ring, part = a.shape[0], a_far.shape[1]
    mine = keep.shape[0]

    @pl.when(step == 0)
    def _():
        places = ring_places(flags[0])
        flip = 2 * flags[1]
        low = (a[...], a_near[...], a_far[:ring, :], a_far[ring:, :])
        for piece, place in zip(low, places):
            rows[rows_at(place ^ flip, ring), :part] = piece
        high = ((b, 0), (b_near, 0), (b_far, 0), (b_far, ring))
        for (piece, start), place in zip(high, places):
            for y in range(Y):
                rows[rows_at((y ^ flip) * X + place, line), part:] = piece[
                    start + y * line : start + (y + 1) * line, :part
                ]

    x = rows[rows_at(step, mine), :]
    own, other = two_products((x[:, :part], x[:, part:]), part, head_keep, head_got)
    store_halves(own, other, keep, send)


def local_kernel(steps, flags, common, policy_keep, policy_got, base_keep, base_got, message, parts, parts_sent):
    step = pl.program_id(0)
    here = rows_at(step, policy_keep.shape[0] // steps)
    policy = policy_keep[here, :] + policy_got[here, :]
    base = base_keep[here, :] + base_got[here, :]
    difference = policy - base
    columns = policy.shape[1] // 2
    policy_peak = jnp.max(policy, axis=1, keepdims=True)
    base_peak = jnp.max(base, axis=1, keepdims=True)
    policy_exp = jnp.exp(policy - policy_peak)
    policy_total = jnp.sum(policy_exp, axis=1, keepdims=True)
    base_total = jnp.sum(jnp.exp(base - base_peak), axis=1, keepdims=True)
    center = jnp.sum(policy_exp * difference, axis=1, keepdims=True) / policy_total
    first = (policy_exp * (difference - center)).astype(BF16)
    second = policy_exp.astype(BF16)
    for i, v in enumerate((first, second)):
        parts[i, here, :] = v
        parts_sent[i, here, :columns] = v[:, columns:]
        parts_sent[i, here, columns:] = v[:, :columns]
    mine = message.shape[1]
    lanes = lax.broadcasted_iota(jnp.int32, (policy.shape[0], mine), 1) + flags[0] * mine
    match = as_column(common[...], step * (mine // steps), mine // steps) == lanes
    values = (
        policy_peak + jnp.log(policy_total),
        base_peak + jnp.log(base_total),
        center,
        policy_peak,
    )
    lines = [jnp.sum(jnp.where(match, v, 0.0), axis=0, keepdims=True) for v in values]
    block = jnp.concatenate(lines + [jnp.zeros((4, mine), F32)], axis=0)

    @pl.when(step == 0)
    def _():
        message[...] = block

    @pl.when(step > 0)
    def _():
        message[...] += block


def merged(messages):
    policy, base, mean = messages[:, 0], messages[:, 1], messages[:, 2]
    policy_peak = jnp.max(policy, axis=0, keepdims=True)
    base_peak = jnp.max(base, axis=0, keepdims=True)
    weights = jnp.exp(policy - policy_peak)
    total = jnp.sum(weights, axis=0, keepdims=True)
    base_total = jnp.sum(jnp.exp(base - base_peak), axis=0, keepdims=True)
    return (
        policy_peak + jnp.log(total),
        base_peak + jnp.log(base_total),
        jnp.sum(weights * mean, axis=0, keepdims=True) / total,
    )


def merge_kernel(flags, messages, out):
    lines = merged(messages[...])
    out[...] = jnp.concatenate([*lines, jnp.zeros((5, out.shape[1]), F32)], axis=0)


def result_kernel(flags, messages, local, out):
    policy, base, mean = merged(messages[...])
    scale = jnp.exp(local[3:4, :] - policy)
    out[...] = jnp.concatenate(
        [scale, local[2:3, :] - mean, mean - policy + base, jnp.zeros((5, out.shape[1]), F32)], axis=0
    )


def sent_kernel(
    line, flags, common, result, result_got, parts, parts_got, head_keep, head_got, low, high, low_rows, high_rows, by_y, by_x
):
    mine = result.shape[1]
    core, flip = flags[0], 2 * flags[1]

    def raw(place):
        return jnp.where((place == 1) | (place == 2), jnp.where(core == 1, 3 - place, place), place)

    for h, (values, source) in enumerate(((result, parts), (result_got, parts_got))):
        first = (core if h == 0 else 1 - core) * mine
        lanes = lax.broadcasted_iota(jnp.int32, (mine, mine), 1) + first
        match = as_column(common[:, h * mine : (h + 1) * mine], 0, mine) == lanes
        scale = jnp.sum(jnp.where(match, values[0:1, :], 0.0), axis=1, keepdims=True)
        shift = jnp.sum(jnp.where(match, values[1:2, :], 0.0), axis=1, keepdims=True)
        grad = (scale * (source[0].astype(F32) + shift * source[1].astype(F32))).astype(BF16)
        for block in range(2 * X):
            y, x = raw((2 * h + block // X) ^ flip), raw(block % X + 0 * core)
            piece = grad[block * line : (block + 1) * line]
            by_y[rows_at(y * X + x, line), :] = piece
            by_x[rows_at(x * Y + y, line), :] = piece
    low[...] = gradient(by_y[mine:, :], head_keep, head_got, 0).astype(BF16)
    high[...] = gradient(by_x[mine:, :], head_keep, head_got, 1).astype(BF16)
    low_rows[...] = by_y[:mine, :]
    high_rows[...] = by_x[:mine, :]


def gradient(rows, head_keep, head_got, which):
    columns = head_keep.shape[1]
    part = head_keep.shape[0] // 2
    span = slice(which * part, (which + 1) * part)
    return lax.dot_general(
        rows[:, :columns], head_keep[span, :], CONTRACT_LAST, preferred_element_type=F32
    ) + lax.dot_general(rows[:, columns:], head_got[span, :], CONTRACT_LAST, preferred_element_type=F32)


def kept_kernel(flags, low_rows, high_rows, head_keep, head_got, low, high):
    low[...] = gradient(low_rows[...], head_keep, head_got, 0)
    high[...] = gradient(high_rows[...], head_keep, head_got, 1)


def on_device(policy_hidden, reference_hidden, head_weight, pair_map, response_mask):
    x0, c0, z0, y0 = (lax.axis_index(name) for name in ("x", "core", "z", "y"))
    second = c0 == 1
    swapped = (c0 ^ (y0 >> 1)) == 1
    own_rows, width = policy_hidden.shape
    half = width // 2
    part = half // 2
    columns = head_weight.shape[1]
    chip_rows = CORES * own_rows
    line = Z * chip_rows
    ring = X * line
    tokens = Y * ring
    mine = tokens // 2

    def side_by_side(first):
        p = lax.dynamic_slice_in_dim(policy_hidden, first, half, 1)
        r = lax.dynamic_slice_in_dim(reference_hidden, first, half, 1)
        return jnp.concatenate([p[:, :part], r[:, :part], p[:, part:], r[:, part:]], 1)

    keep = side_by_side(c0 * half)
    got = exchange(side_by_side((1 - c0) * half), across_cores)
    rows = jnp.concatenate([jnp.where(second, got, keep), jnp.where(second, keep, got)], 0)
    rows, head_weight = lax.optimization_barrier((rows, head_weight))
    flags = jnp.stack([c0, c0 ^ (y0 >> 1)]).astype(jnp.int32)
    head_shape = jax.ShapeDtypeStruct((half, columns), BF16)
    slot = jnp.arange(tokens, dtype=jnp.int32)[None]

    def raw(j):
        return jnp.where(second, jnp.where(j == 0, 0, jnp.where(j == 3, 1, j + 1)), gray(j))

    sr, sc = slot % own_rows, (slot // own_rows) % CORES
    sz = z_offset((slot // chip_rows) % Z) ^ z0
    sx = gray((slot // line) % X) ^ x0
    sy = gray((slot // ring) ^ jnp.where(swapped, 2, 0)) ^ y0
    own_token = flat(sx, sc, sz, sy) * own_rows + sr
    rows = gather_z(rows, Z_STEPS[:1])
    rows, own_token = lax.optimization_barrier((rows, own_token))
    every = jnp.arange(tokens, dtype=jnp.int32)
    partner = jnp.sum(jnp.where(own_token[0][:, None] == every[None], pair_map[None], 0), axis=1)[None]
    rows = gather_z(rows, Z_STEPS[1:2])
    rows, partner, head_weight = lax.optimization_barrier((rows, partner, head_weight))
    head_keep, head_send = run(
        take_head,
        "take_head",
        flags,
        (head_weight,),
        [head_shape, head_shape],
        in_specs=[pl.BlockSpec(memory_space=pltpu.HBM)],
        scratch=[pltpu.SemaphoreType.DMA] * 2,
    )
    rows = gather_z(rows, Z_STEPS[2:])
    rows, head_keep, head_send = lax.optimization_barrier((rows, head_keep, head_send))
    head = (head_keep, exchange(head_send, across_cores))
    pr, pdev = partner % own_rows, partner // own_rows
    py, pz, pc, px = pdev % Y, (pdev // Y) % Z, (pdev // (Y * Z)) % CORES, pdev // (Y * Z * CORES)
    tail = (z_slot(pz ^ z0) * CORES + pc) * own_rows + pr
    low_place = ((raw(py ^ y0) * X + gray(px ^ x0)) * line + tail).astype(F32)
    high_place = ((raw(px ^ x0) * Y + gray(py ^ y0)) * line + tail).astype(F32)
    common = (((sy * X + sx) * Z + sz) * chip_rows + sc * own_rows + sr).astype(F32)

    spans = [(rows[:, part:half], rows[:, half + part :]), (rows[:, :part], rows[:, half : half + part])]
    gathered = []
    for low, high in spans:
        low_near, high_near = ring_near(low, along_x), ring_near(high, along_y)
        low_far, high_far = ring_far(low, low_near, along_x), ring_far(high, high_near, along_y)
        a, b = run(
            order_kernel,
            "order",
            flags,
            (low, low_near, low_far, high, high_near, high_far),
            [jax.ShapeDtypeStruct((ring, part), BF16)] * 2,
        )
        a_near, b_near = ring_near(a, along_y), ring_near(b, along_x)
        a_far, b_far = ring_far(a, a_near, along_y), ring_far(b, b_near, along_x)
        gathered.append((a, a_near, a_far, b, b_near, b_far))
    base, policy = gathered

    logits = [jax.ShapeDtypeStruct((mine, 2 * columns), F32)] * 2
    flops = 4 * tokens * half * columns
    base_keep, base_send = run(
        base_kernel,
        "base_logits",
        flags,
        (low_place, high_place, *base, *head),
        logits,
        grid=(2,),
        flops=2 * flops,
    )
    base_got = exchange(base_send, across_cores)
    policy_keep, policy_send = run(
        functools.partial(policy_kernel, line),
        "policy_logits",
        flags,
        (*policy, *head),
        logits,
        grid=(2,),
        scratch=[pltpu.VMEM((tokens, half), BF16)],
        flops=flops,
    )
    policy_got = exchange(policy_send, across_cores)

    steps = 4
    message_shape = jax.ShapeDtypeStruct((8, mine), F32)
    parts_shape = jax.ShapeDtypeStruct((2, mine, 2 * columns), BF16)
    message, parts, parts_sent = run(
        functools.partial(local_kernel, steps),
        "local_sums",
        flags,
        (common[:, :mine], policy_keep, policy_got, base_keep, base_got),
        [message_shape, parts_shape, parts_shape],
        grid=(steps,),
    )
    parts_got = exchange(parts_sent, across_cores)

    gathered = message
    for step in Z_STEPS:
        gathered = jnp.concatenate([gathered, exchange(gathered, along_z(step))], 0)
    (line_message,) = run(merge_kernel, "merge", flags, (gathered.reshape(Z, 8, mine),), [message_shape])
    everyone = lax.all_to_all(jnp.broadcast_to(line_message[None], (X * Y, 8, mine)), ("x", "y"), 0, 0)
    (result,) = run(result_kernel, "result", flags, (everyone, message), [message_shape])
    result_got = exchange(result, across_cores)

    rows_shape = jax.ShapeDtypeStruct((mine, 2 * columns), BF16)
    sent_shape = jax.ShapeDtypeStruct((mine, part), BF16)
    kept_shape = jax.ShapeDtypeStruct((mine, part), F32)
    operands = (common, result, result_got, parts, parts_got)
    low_sent, high_sent, low_rows, high_rows = run(
        functools.partial(sent_kernel, line),
        "gradient_sent",
        flags,
        (*operands, *head),
        [sent_shape, sent_shape, rows_shape, rows_shape],
        scratch=[pltpu.VMEM((tokens, 2 * columns), BF16)] * 2,
        flops=flops // 2,
    )
    low_got, high_got = exchange(low_sent, along_y(3, 1)), exchange(high_sent, along_x(3, 1))
    low_kept, high_kept = run(
        kept_kernel,
        "gradient_kept",
        flags,
        (low_rows, high_rows, *head),
        [kept_shape, kept_shape],
        flops=flops // 2,
    )
    low_total = low_kept + low_got.astype(F32)
    high_total = high_kept + high_got.astype(F32)
    low_total = scatter_step(low_total, along_y(1, 3))
    high_total = scatter_step(high_total, along_x(1, 3))
    low_total = scatter_step(scatter_step(low_total, along_x(3, 1)), along_x(1, 3))
    high_total = scatter_step(scatter_step(high_total, along_y(3, 1)), along_y(1, 3))
    total = jnp.concatenate([low_total, high_total], 1)
    for step in Z_STEPS[::-1]:
        total = scatter_step(total, along_z(step))

    keep = lax.dynamic_slice_in_dim(total, c0 * own_rows, own_rows, 0)
    got = exchange(lax.dynamic_slice_in_dim(total, (1 - c0) * own_rows, own_rows, 0), across_cores)
    grad = jnp.concatenate([jnp.where(second, got, keep), jnp.where(second, keep, got)], 1)
    position = ((y0 * X + x0) * Z + z0) * chip_rows + c0 * own_rows
    divergence = jnp.where(second, jnp.stack([result_got[2], result[2]]), jnp.stack([result[2], result_got[2]]))
    own_divergence = lax.dynamic_slice_in_dim(divergence.reshape(-1), position, own_rows, 0)
    weight = response_mask.astype(F32)
    return (weight * own_divergence, (weight[:, None] * grad).astype(BF16))


def solution(mesh):
    chips = Mesh(mesh.devices.reshape(X, CORES, Z, Y), AXES)
    return jax.shard_map(
        on_device,
        mesh=chips,
        in_specs=(P(AXES, None), P(AXES, None), P(None, AXES), P(), P(AXES)),
        out_specs=(P(AXES), P(AXES, None)),
        check_vma=False,
    )
```

```python
import functools

import jax
import jax.numpy as jnp
from jax import lax
from jax.experimental import pallas as pl
from jax.experimental.pallas import tpu as pltpu
from jax.sharding import Mesh, PartitionSpec as P

X, CORES, Z, Y = 4, 2, 8, 4
AXES = ("x", "core", "z", "y")
F32, BF16 = jnp.float32, jnp.bfloat16


def flat(x, c, z, y):
    return ((x * CORES + c) * Z + z) * Y + y


def exchange(value, partner):
    pairs = [
        (flat(x, c, z, y), flat(*partner(x, c, z, y)))
        for x in range(X)
        for c in range(CORES)
        for z in range(Z)
        for y in range(Y)
    ]
    return lax.ppermute(value, AXES, pairs)


def along_x(first, second):
    return lambda x, c, z, y: (x ^ (second if c else first), c, z, y)


def along_y(first, second):
    return lambda x, c, z, y: (x, c, z, y ^ (second if c else first))


def along_z(step):
    return lambda x, c, z, y: (x, c, z ^ step, y)


def across_cores(x, c, z, y):
    return (x, 1 - c, z, y)


Z_STEPS = (2, 6, 1)


def gray(j):
    return j ^ (j >> 1)


def z_slot(j):
    return (((j >> 1) ^ (j >> 2)) & 1) | ((j >> 1) & 2) | ((j & 1) << 2)


def z_offset(slot):
    return (slot >> 2) ^ ((slot & 1) * 2) ^ (((slot >> 1) & 1) * 6)


def gather_z(rows, steps):
    for step in steps:
        rows = jnp.concatenate([rows, exchange(rows, along_z(step))], 0)
    return rows


def ring_near(rows, along):
    return exchange(rows, along(1, 3))


def ring_far(rows, near, along):
    return exchange(jnp.concatenate([rows, near], 0), along(3, 1))


def scatter_step(total, partner):
    half = total.shape[0] // 2
    return total[:half] + exchange(total[half:].astype(BF16), partner).astype(F32)


CONTRACT_LAST = (((1,), (1,)), ((), ()))
VMEM_LIMIT = 20 * 1024 * 1024


WHOLE = pl.BlockSpec(memory_space=pltpu.VMEM)


def run(kernel, name, flags, operands, outputs, grid=(1,), scratch=(), in_specs=None, flops=0):
    bytes_accessed = sum(v.size * v.dtype.itemsize for v in (*operands, *outputs))
    return pl.pallas_call(
        kernel,
        out_shape=outputs,
        grid_spec=pltpu.PrefetchScalarGridSpec(
            num_scalar_prefetch=1,
            grid=grid,
            in_specs=in_specs or [WHOLE] * len(operands),
            out_specs=[WHOLE] * len(outputs),
            scratch_shapes=list(scratch),
        ),
        compiler_params=pltpu.CompilerParams(vmem_limit_bytes=VMEM_LIMIT),
        cost_estimate=pl.CostEstimate(flops=flops, bytes_accessed=bytes_accessed, transcendentals=0),
        name=name,
    )(flags, *operands)


def ring_places(core):
    return (0, 1 + core, 2 - core, 3)


def rows_at(block, count):
    return pl.ds(pl.multiple_of(block * count, count), count)


def as_column(row, start, count):
    here = lax.broadcasted_iota(jnp.int32, (count, row.shape[1]), 0) + start
    lanes = lax.broadcasted_iota(jnp.int32, (count, row.shape[1]), 1)
    return jnp.sum(jnp.where(here == lanes, row, 0.0), axis=1, keepdims=True).astype(jnp.int32)


def order_kernel(flags, low, low_near, low_far, high, high_near, high_far, a, b):
    line = low.shape[0]
    places = ring_places(flags[0])
    for rows, near, far, out in ((low, low_near, low_far, a), (high, high_near, high_far, b)):
        for (piece, start), place in zip(((rows, 0), (near, 0), (far, 0), (far, line)), places):
            out[rows_at(place, line), :] = piece[start : start + line, :]


def take_head(flags, head, keep, send, keep_done, send_done):
    half = keep.shape[0]
    copies = [
        pltpu.make_async_copy(head.at[rows_at(index, half), :], half_ref, done)
        for index, half_ref, done in ((flags[0], keep, keep_done), (1 - flags[0], send, send_done))
    ]
    for copy in copies:
        copy.start()
    for copy in copies:
        copy.wait()


def two_products(x, part, head_keep, head_got):
    def product(head):
        return jnp.dot(x[0], head[:part, :], preferred_element_type=F32) + jnp.dot(
            x[1], head[part:, :], preferred_element_type=F32
        )

    return product(head_keep), product(head_got)


def store_halves(own, other, keep, send):
    columns = own.shape[1]
    step = pl.program_id(0)

    @pl.when(step == 0)
    def _():
        keep[:, :columns] = own
        keep[:, columns:] = other

    @pl.when(step == 1)
    def _():
        send[:, :columns] = other
        send[:, columns:] = own


def base_kernel(
    flags, low_place, high_place, a, a_near, a_far, b, b_near, b_far, head_keep, head_got, keep, send
):
    count = keep.shape[0]
    first = pl.program_id(0) * count

    def pick(place, rows, near, far):
        ring, part = far.shape[0] // 2, far.shape[1]
        lanes = lax.broadcasted_iota(jnp.int32, (count, 4 * ring), 1)
        one_hot = jnp.where(as_column(place[...], first, count) == lanes, 1.0, 0.0).astype(BF16)
        total = jnp.dot(one_hot[:, :ring], rows[...], preferred_element_type=F32)
        total += jnp.dot(one_hot[:, ring : 2 * ring], near[...], preferred_element_type=F32)
        total += jnp.dot(one_hot[:, 2 * ring :], far[...], preferred_element_type=F32)
        return total.astype(BF16)

    x = (pick(low_place, a, a_near, a_far), pick(high_place, b, b_near, b_far))
    own, other = two_products(x, a_far.shape[1], head_keep, head_got)
    store_halves(own, other, keep, send)


def policy_kernel(line, flags, a, a_near, a_far, b, b_near, b_far, head_keep, head_got, keep, send, rows):
    step = pl.program_id(0)
    ring, part = a.shape[0], a_far.shape[1]
    mine = keep.shape[0]

    @pl.when(step == 0)
    def _():
        places = ring_places(flags[0])
        flip = 2 * flags[1]
        low = (a[...], a_near[...], a_far[:ring, :], a_far[ring:, :])
        for piece, place in zip(low, places):
            rows[rows_at(place ^ flip, ring), :part] = piece
        high = ((b, 0), (b_near, 0), (b_far, 0), (b_far, ring))
        for (piece, start), place in zip(high, places):
            for y in range(Y):
                rows[rows_at((y ^ flip) * X + place, line), part:] = piece[
                    start + y * line : start + (y + 1) * line, :part
                ]

    x = rows[rows_at(step, mine), :]
    own, other = two_products((x[:, :part], x[:, part:]), part, head_keep, head_got)
    store_halves(own, other, keep, send)


def local_kernel(steps, flags, common, policy_keep, policy_got, base_keep, base_got, message, parts, parts_sent):
    step = pl.program_id(0)
    here = rows_at(step, policy_keep.shape[0] // steps)
    policy = policy_keep[here, :] + policy_got[here, :]
    base = base_keep[here, :] + base_got[here, :]
    difference = policy - base
    columns = policy.shape[1] // 2
    policy_peak = jnp.max(policy, axis=1, keepdims=True)
    base_peak = jnp.max(base, axis=1, keepdims=True)
    policy_exp = jnp.exp(policy - policy_peak)
    policy_total = jnp.sum(policy_exp, axis=1, keepdims=True)
    base_total = jnp.sum(jnp.exp(base - base_peak), axis=1, keepdims=True)
    center = jnp.sum(policy_exp * difference, axis=1, keepdims=True) / policy_total
    first = (policy_exp * (difference - center)).astype(BF16)
    second = policy_exp.astype(BF16)
    for i, v in enumerate((first, second)):
        parts[i, here, :] = v
        parts_sent[i, here, :columns] = v[:, columns:]
        parts_sent[i, here, columns:] = v[:, :columns]
    mine = message.shape[1]
    lanes = lax.broadcasted_iota(jnp.int32, (policy.shape[0], mine), 1) + flags[0] * mine
    match = as_column(common[...], step * (mine // steps), mine // steps) == lanes
    values = (
        policy_peak + jnp.log(policy_total),
        base_peak + jnp.log(base_total),
        center,
        policy_peak,
    )
    lines = [jnp.sum(jnp.where(match, v, 0.0), axis=0, keepdims=True) for v in values]
    block = jnp.concatenate(lines + [jnp.zeros((4, mine), F32)], axis=0)

    @pl.when(step == 0)
    def _():
        message[...] = block

    @pl.when(step > 0)
    def _():
        message[...] += block


def merged(messages):
    policy, base, mean = messages[:, 0], messages[:, 1], messages[:, 2]
    policy_peak = jnp.max(policy, axis=0, keepdims=True)
    base_peak = jnp.max(base, axis=0, keepdims=True)
    weights = jnp.exp(policy - policy_peak)
    total = jnp.sum(weights, axis=0, keepdims=True)
    base_total = jnp.sum(jnp.exp(base - base_peak), axis=0, keepdims=True)
    return (
        policy_peak + jnp.log(total),
        base_peak + jnp.log(base_total),
        jnp.sum(weights * mean, axis=0, keepdims=True) / total,
    )


def merge_kernel(flags, messages, out):
    lines = merged(messages[...])
    out[...] = jnp.concatenate([*lines, jnp.zeros((5, out.shape[1]), F32)], axis=0)


def result_kernel(flags, messages, local, out):
    policy, base, mean = merged(messages[...])
    scale = jnp.exp(local[3:4, :] - policy)
    out[...] = jnp.concatenate(
        [scale, local[2:3, :] - mean, mean - policy + base, jnp.zeros((5, out.shape[1]), F32)], axis=0
    )


def sent_kernel(
    line, flags, common, result, result_got, parts, parts_got, head_keep, head_got, low, high, low_rows, high_rows, by_y, by_x
):
    mine = result.shape[1]
    core, flip = flags[0], 2 * flags[1]

    def raw(place):
        return jnp.where((place == 1) | (place == 2), jnp.where(core == 1, 3 - place, place), place)

    for h, (values, source) in enumerate(((result, parts), (result_got, parts_got))):
        first = (core if h == 0 else 1 - core) * mine
        lanes = lax.broadcasted_iota(jnp.int32, (mine, mine), 1) + first
        match = as_column(common[:, h * mine : (h + 1) * mine], 0, mine) == lanes
        scale = jnp.sum(jnp.where(match, values[0:1, :], 0.0), axis=1, keepdims=True)
        shift = jnp.sum(jnp.where(match, values[1:2, :], 0.0), axis=1, keepdims=True)
        grad = (scale * (source[0].astype(F32) + shift * source[1].astype(F32))).astype(BF16)
        for block in range(2 * X):
            y, x = raw((2 * h + block // X) ^ flip), raw(block % X + 0 * core)
            piece = grad[block * line : (block + 1) * line]
            by_y[rows_at(y * X + x, line), :] = piece
            by_x[rows_at(x * Y + y, line), :] = piece
    low[...] = gradient(by_y[mine:, :], head_keep, head_got, 0).astype(BF16)
    high[...] = gradient(by_x[mine:, :], head_keep, head_got, 1).astype(BF16)
    low_rows[...] = by_y[:mine, :]
    high_rows[...] = by_x[:mine, :]


def gradient(rows, head_keep, head_got, which):
    columns = head_keep.shape[1]
    part = head_keep.shape[0] // 2
    span = slice(which * part, (which + 1) * part)
    return lax.dot_general(
        rows[:, :columns], head_keep[span, :], CONTRACT_LAST, preferred_element_type=F32
    ) + lax.dot_general(rows[:, columns:], head_got[span, :], CONTRACT_LAST, preferred_element_type=F32)


def kept_kernel(flags, low_rows, high_rows, head_keep, head_got, low, high):
    low[...] = gradient(low_rows[...], head_keep, head_got, 0)
    high[...] = gradient(high_rows[...], head_keep, head_got, 1)


def on_device(policy_hidden, reference_hidden, head_weight, pair_map, response_mask):
    x0, c0, z0, y0 = (lax.axis_index(name) for name in ("x", "core", "z", "y"))
    second = c0 == 1
    swapped = (c0 ^ (y0 >> 1)) == 1
    own_rows, width = policy_hidden.shape
    half = width // 2
    part = half // 2
    columns = head_weight.shape[1]
    chip_rows = CORES * own_rows
    line = Z * chip_rows
    ring = X * line
    tokens = Y * ring
    mine = tokens // 2

    def side_by_side(first):
        p = lax.dynamic_slice_in_dim(policy_hidden, first, half, 1)
        r = lax.dynamic_slice_in_dim(reference_hidden, first, half, 1)
        return jnp.concatenate([p[:, :part], r[:, :part], p[:, part:], r[:, part:]], 1)

    keep = side_by_side(c0 * half)
    got = exchange(side_by_side((1 - c0) * half), across_cores)
    rows = jnp.concatenate([jnp.where(second, got, keep), jnp.where(second, keep, got)], 0)
    flags = jnp.stack([c0, c0 ^ (y0 >> 1)]).astype(jnp.int32)
    head_shape = jax.ShapeDtypeStruct((half, columns), BF16)
    slot = jnp.arange(tokens, dtype=jnp.int32)[None]

    def raw(j):
        return jnp.where(second, jnp.where(j == 0, 0, jnp.where(j == 3, 1, j + 1)), gray(j))

    sr, sc = slot % own_rows, (slot // own_rows) % CORES
    sz = z_offset((slot // chip_rows) % Z) ^ z0
    sx = gray((slot // line) % X) ^ x0
    sy = gray((slot // ring) ^ jnp.where(swapped, 2, 0)) ^ y0
    own_token = flat(sx, sc, sz, sy) * own_rows + sr
    rows = gather_z(rows, Z_STEPS[:1])
    rows, own_token = lax.optimization_barrier((rows, own_token))
    every = jnp.arange(tokens, dtype=jnp.int32)
    partner = jnp.sum(jnp.where(own_token[0][:, None] == every[None], pair_map[None], 0), axis=1)[None]
    rows = gather_z(rows, Z_STEPS[1:2])
    rows, partner = lax.optimization_barrier((rows, partner))
    head_keep, head_send = run(
        take_head,
        "take_head",
        flags,
        (head_weight,),
        [head_shape, head_shape],
        in_specs=[pl.BlockSpec(memory_space=pltpu.HBM)],
        scratch=[pltpu.SemaphoreType.DMA] * 2,
    )
    rows = gather_z(rows, Z_STEPS[2:])
    rows, head_keep, head_send = lax.optimization_barrier((rows, head_keep, head_send))
    head = (head_keep, exchange(head_send, across_cores))
    pr, pdev = partner % own_rows, partner // own_rows
    py, pz, pc, px = pdev % Y, (pdev // Y) % Z, (pdev // (Y * Z)) % CORES, pdev // (Y * Z * CORES)
    tail = (z_slot(pz ^ z0) * CORES + pc) * own_rows + pr
    low_place = ((raw(py ^ y0) * X + gray(px ^ x0)) * line + tail).astype(F32)
    high_place = ((raw(px ^ x0) * Y + gray(py ^ y0)) * line + tail).astype(F32)
    common = (((sy * X + sx) * Z + sz) * chip_rows + sc * own_rows + sr).astype(F32)

    spans = [(rows[:, part:half], rows[:, half + part :]), (rows[:, :part], rows[:, half : half + part])]
    gathered = []
    for low, high in spans:
        low_near, high_near = ring_near(low, along_x), ring_near(high, along_y)
        low_far, high_far = ring_far(low, low_near, along_x), ring_far(high, high_near, along_y)
        a, b = run(
            order_kernel,
            "order",
            flags,
            (low, low_near, low_far, high, high_near, high_far),
            [jax.ShapeDtypeStruct((ring, part), BF16)] * 2,
        )
        a_near, b_near = ring_near(a, along_y), ring_near(b, along_x)
        a_far, b_far = ring_far(a, a_near, along_y), ring_far(b, b_near, along_x)
        gathered.append((a, a_near, a_far, b, b_near, b_far))
    base, policy = gathered

    logits = [jax.ShapeDtypeStruct((mine, 2 * columns), F32)] * 2
    flops = 4 * tokens * half * columns
    base_keep, base_send = run(
        base_kernel,
        "base_logits",
        flags,
        (low_place, high_place, *base, *head),
        logits,
        grid=(2,),
        flops=2 * flops,
    )
    base_got = exchange(base_send, across_cores)
    policy_keep, policy_send = run(
        functools.partial(policy_kernel, line),
        "policy_logits",
        flags,
        (*policy, *head),
        logits,
        grid=(2,),
        scratch=[pltpu.VMEM((tokens, half), BF16)],
        flops=flops,
    )
    policy_got = exchange(policy_send, across_cores)

    steps = 4
    message_shape = jax.ShapeDtypeStruct((8, mine), F32)
    parts_shape = jax.ShapeDtypeStruct((2, mine, 2 * columns), BF16)
    message, parts, parts_sent = run(
        functools.partial(local_kernel, steps),
        "local_sums",
        flags,
        (common[:, :mine], policy_keep, policy_got, base_keep, base_got),
        [message_shape, parts_shape, parts_shape],
        grid=(steps,),
    )
    parts_got = exchange(parts_sent, across_cores)

    gathered = message
    for step in Z_STEPS:
        gathered = jnp.concatenate([gathered, exchange(gathered, along_z(step))], 0)
    (line_message,) = run(merge_kernel, "merge", flags, (gathered.reshape(Z, 8, mine),), [message_shape])
    everyone = lax.all_to_all(jnp.broadcast_to(line_message[None], (X * Y, 8, mine)), ("x", "y"), 0, 0)
    (result,) = run(result_kernel, "result", flags, (everyone, message), [message_shape])
    result_got = exchange(result, across_cores)

    rows_shape = jax.ShapeDtypeStruct((mine, 2 * columns), BF16)
    sent_shape = jax.ShapeDtypeStruct((mine, part), BF16)
    kept_shape = jax.ShapeDtypeStruct((mine, part), F32)
    operands = (common, result, result_got, parts, parts_got)
    low_sent, high_sent, low_rows, high_rows = run(
        functools.partial(sent_kernel, line),
        "gradient_sent",
        flags,
        (*operands, *head),
        [sent_shape, sent_shape, rows_shape, rows_shape],
        scratch=[pltpu.VMEM((tokens, 2 * columns), BF16)] * 2,
        flops=flops // 2,
    )
    low_got, high_got = exchange(low_sent, along_y(3, 1)), exchange(high_sent, along_x(3, 1))
    low_kept, high_kept = run(
        kept_kernel,
        "gradient_kept",
        flags,
        (low_rows, high_rows, *head),
        [kept_shape, kept_shape],
        flops=flops // 2,
    )
    low_total = low_kept + low_got.astype(F32)
    high_total = high_kept + high_got.astype(F32)
    low_total = scatter_step(low_total, along_y(1, 3))
    high_total = scatter_step(high_total, along_x(1, 3))
    low_total = scatter_step(scatter_step(low_total, along_x(3, 1)), along_x(1, 3))
    high_total = scatter_step(scatter_step(high_total, along_y(3, 1)), along_y(1, 3))
    total = jnp.concatenate([low_total, high_total], 1)
    for step in Z_STEPS[::-1]:
        total = scatter_step(total, along_z(step))

    keep = lax.dynamic_slice_in_dim(total, c0 * own_rows, own_rows, 0)
    got = exchange(lax.dynamic_slice_in_dim(total, (1 - c0) * own_rows, own_rows, 0), across_cores)
    grad = jnp.concatenate([jnp.where(second, got, keep), jnp.where(second, keep, got)], 1)
    position = ((y0 * X + x0) * Z + z0) * chip_rows + c0 * own_rows
    divergence = jnp.where(second, jnp.stack([result_got[2], result[2]]), jnp.stack([result[2], result_got[2]]))
    own_divergence = lax.dynamic_slice_in_dim(divergence.reshape(-1), position, own_rows, 0)
    weight = response_mask.astype(F32)
    return (weight * own_divergence, (weight[:, None] * grad).astype(BF16))


def solution(mesh):
    chips = Mesh(mesh.devices.reshape(X, CORES, Z, Y), AXES)
    return jax.shard_map(
        on_device,
        mesh=chips,
        in_specs=(P(AXES, None), P(AXES, None), P(None, AXES), P(), P(AXES)),
        out_specs=(P(AXES), P(AXES, None)),
        check_vma=False,
    )
```
